256 devices in a mesh: dp: 16 (over y, z_hi, core), expert: 16 (over x, z_lo).
Axes of the slice: x: 4, y: 4, z: 8 (z_hi: 2, z_lo: 4; z = z_hi * 4 + z_lo), core: 2. Of those that a mesh axis runs over, the one named last changes fastest.
Arguments:
- tokens: bfloat16 [512, 4096], P('dp'), may hold values from -6 to 6
- cotangent: bfloat16 [512, 4096], P('dp'), may hold values from -0.29882812 to 0.29882812
- logits: float32 [512, 64], P('dp'), may hold values from 0 to 320
- routes: int32 [512, 8], P('dp'), may hold values from 0 to 63, as said below
- gate_weight: bfloat16 [64, 1536, 4096], P('expert', 'dp'), may hold values from -0.09375 to 0.09375
- up_weight: bfloat16 [64, 1536, 4096], P('expert', 'dp'), may hold values from -0.09375 to 0.09375
- down_weight: bfloat16 [64, 1536, 4096], P('expert', 'dp'), may hold values from -0.15625 to 0.15625
Outputs:
- logit_grad: float32 [512, 64], P('dp')
- router_grad: float32 [4096, 64], P('dp')
The draws below stay inside these ranges and needn't reach their ends.
Inputs may be any that keep to these rules, and one draw needn't show every extreme that they name: `routes`: each row names 8 different experts.
All inputs are finite; a program needn't handle non-finite values.
Results may differ from the reference program's by a relative error of at most 0.0028.
Values may be sent and summed in bfloat16 or wider, within the bound.
A program may use at most 64 MiB of HBM per device.

```python
import jax
import jax.numpy as jnp
from jax import lax

D = 4096
FF = 1536
TOP = 8
EXPERTS = 64
TOKENS = 512


def pick_routes(key):
    ranks = jax.random.randint(key, (TOKENS, EXPERTS), 0, 65536) * EXPERTS
    ranks = ranks + jnp.arange(EXPERTS, dtype=jnp.int32)[None, :]
    return lax_top(ranks)


def lax_top(ranks):
    return jax.lax.top_k(ranks, TOP)[1].astype(jnp.int32)


def draw_routes(key, part):
    return pick_routes(key)


def draw_logits(key, part):
    picked = pick_routes(key)
    key = jax.random.fold_in(key, 7)
    experts_range = jnp.arange(EXPERTS, dtype=jnp.int32)
    chosen = jnp.sum((picked[:, :, None] == experts_range[None, None, :]).astype(jnp.float32), axis=1)
    base = jnp.clip(0.5 * jax.random.normal(key, (TOKENS, EXPERTS), jnp.float32), -1.0, 1.0)
    return 1.5 + base + 2.0 * chosen


def levels(stream_key, dims, cuts, smallest, high):
    gain = 1.0
    for position, parts in cuts:
        heights = jax.random.uniform(jax.random.fold_in(jax.random.fold_in(stream_key, 6), position), (parts,), jnp.float32, smallest / len(cuts), high / len(cuts))
        gain = gain * jnp.repeat(jnp.exp(heights), dims[position] // parts).reshape((-1,) + (1,) * (len(dims) - 1 - position))
    return gain


def scatter_about(own_key, shape, scale, limit, cuts=(), kind=jnp.bfloat16):
    drawn = jax.random.normal(own_key, shape, jnp.float32) * scale
    if len(cuts) > 0:
        drawn = levels(own_key, shape, cuts, -0.22, 0.18) * drawn
    return jnp.clip(drawn, min=-limit, max=limit).astype(kind)


def setup_inputs(seed: int = 0) -> dict:
    streams_of = jax.random.split(jax.random.key(seed), 8)
    tokens = scatter_about(streams_of[0], (TOKENS, D), 1.0, 6.0, ((0, 16),))
    cotangent = scatter_about(streams_of[1], (TOKENS, D), 0.05, 0.29882812, ((0, 16),))
    logits = draw_logits(jax.random.fold_in(streams_of[7], 71), 0)
    routes = draw_routes(jax.random.fold_in(streams_of[7], 71), 0)
    gate_weight = scatter_about(streams_of[4], (EXPERTS, FF, D), D ** -0.5, 0.09375, ((0, 16), (1, 16)))
    up_weight = scatter_about(streams_of[5], (EXPERTS, FF, D), D ** -0.5, 0.09375, ((0, 16), (1, 16)))
    down_weight = scatter_about(streams_of[6], (EXPERTS, FF, D), FF ** -0.5, 0.15625, ((0, 16), (1, 16)))
    return dict(tokens=tokens, cotangent=cotangent, logits=logits, routes=routes, gate_weight=gate_weight, up_weight=up_weight, down_weight=down_weight)


def expert_scores(tokens, cotangent, weights):
    gate_rows, up_rows, down_rows = weights
    gate_pre = jnp.dot(tokens, gate_rows.T, preferred_element_type=jnp.float32)
    up_pre = jnp.dot(tokens, up_rows.T, preferred_element_type=jnp.float32)
    hidden = jax.nn.silu(gate_pre) * up_pre
    paired = jnp.dot(cotangent, down_rows.T, preferred_element_type=jnp.float32)
    return jnp.sum(hidden * paired, axis=1)


def reference(tokens, cotangent, logits, routes, gate_weight, up_weight, down_weight):
    scores = lax.map(lambda weights: expert_scores(tokens, cotangent, weights), (gate_weight, up_weight, down_weight)).T
    shifted = logits - jnp.max(logits, axis=1, keepdims=True)
    raised = jnp.exp(shifted)
    probs = raised / jnp.sum(raised, axis=1, keepdims=True)
    experts_range = jnp.arange(EXPERTS, dtype=jnp.int32)
    chosen = jnp.sum((routes[:, :, None] == experts_range[None, None, :]).astype(jnp.float32), axis=1)
    mass = jnp.sum(probs * chosen, axis=1, keepdims=True)
    weighted = jnp.sum(probs * chosen * scores, axis=1, keepdims=True)
    prob_grad = scores / mass - chosen * weighted / (mass * mass)
    logit_grad = probs * (prob_grad - jnp.sum(probs * prob_grad, axis=1, keepdims=True))
    grad_bf = logit_grad.astype(jnp.bfloat16)
    router_grad = jnp.dot(tokens.T, grad_bf, preferred_element_type=jnp.float32)
    return logit_grad, router_grad
```

```python
import jax
import jax.numpy as jnp
from jax import lax
from jax.experimental import pallas as pl
from jax.experimental.pallas import tpu as pltpu
from jax.sharding import PartitionSpec as P

MESH = pl.DeviceIdType.MESH
MIB = 1024 * 1024
NT = (((1,), (1,)), ((), ()))


class Sems:
    def __init__(self, ref):
        self.ref, self.names = ref, {}

    def __getitem__(self, name):
        return self.ref.at[self.names.setdefault(name, len(self.names))]


def kernel(tok, cot, logits, routes, gate, up, down, lg_out, rg_out,
           xg, wgu, wd, accx, accg, lmat, probs, chosen, part, got1, got2, lgc, turned,
           load_sem, send_ref, recv_ref):
    d = lax.axis_index("dp")
    e = lax.axis_index("expert")
    y, zh, c = d // 4, (d // 2) % 2, d % 2
    x, zl = e // 4, e % 4
    z = zh * 4 + zl
    par = x % 2
    send_sem, recv_sem = Sems(send_ref), Sems(recv_ref)

    def dev(x_, y_, z_, c_):
        return ((y_ * 2 + z_ // 4) * 2 + c_, x_ * 4 + z_ % 4)

    xp, xm = dev((x + 1) % 4, y, z, c), dev((x + 3) % 4, y, z, c)
    yp, ym = dev(x, (y + 1) % 4, z, c), dev(x, (y + 3) % 4, z, c)
    zp, zm = dev(x, y, (z + 1) % 8, c), dev(x, y, (z + 7) % 8, c)
    low = zl < 2
    outn = tuple(jnp.where(low, a, b) for a, b in zip(zm, zp))
    inn = tuple(jnp.where(low, a, b) for a, b in zip(zp, zm))
    sib = dev(x, y, z, 1 - c)
    edge = (zl == 0) | (zl == 3)

    own_x = pltpu.make_async_copy(tok, xg.at[0, zh, c, y], load_sem.at[0])
    own_g = pltpu.make_async_copy(cot, xg.at[1, zh, c, y], load_sem.at[1])
    w_gate = pltpu.make_async_copy(gate, wgu.at[pl.ds(0, 384)], load_sem.at[2])
    w_up = pltpu.make_async_copy(up, wgu.at[pl.ds(384, 384)], load_sem.at[3])
    w_down = pltpu.make_async_copy(down, wd, load_sem.at[4])
    own_x.start()
    own_g.start()
    barrier = pltpu.get_barrier_semaphore()
    for k in range(1, 16):
        pl.semaphore_signal(barrier, inc=1, device_id=((d + k) % 16, e), device_id_type=MESH)
    for k in range(1, 16):
        pl.semaphore_signal(barrier, inc=1, device_id=(d, (e + k) % 16), device_id_type=MESH)
    for to in (zp, zm):
        pl.semaphore_signal(barrier, inc=1, device_id=to, device_id_type=MESH)
    w_gate.start()
    w_up.start()
    w_down.start()
    lane = lax.broadcasted_iota(jnp.int32, (32, 128), 1)
    picked = jnp.zeros((32, 128), jnp.float32)
    for k in range(8):
        picked += (routes[:, k : k + 1] == lane - 64).astype(jnp.float32)
    lmat[zh, c, y] = picked
    lmat[zh, c, y, :, pl.ds(0, 64)] = logits[...]
    own_x.wait()
    own_g.wait()
    pl.semaphore_wait(barrier, 32)

    pending = []

    def ship(ref, to, name_here, name_there):
        cp = pltpu.make_async_remote_copy(
            ref, ref, send_sem[name_here], recv_sem[name_there], device_id=to, device_id_type=MESH)
        cp.start()
        return cp

    def send(ref, to, name_here, name_there):
        pending.append(ship(ref, to, name_here, name_there))

    def landed(ref, name):
        pltpu.make_async_remote_copy(
            ref, ref, send_sem[("x+", 0, "m", 0)], recv_sem[name], device_id=sib, device_id_type=MESH).wait_recv()

    def piece(dz, dy, rel, s):
        zz = zh if dz == 0 else 1 - zh
        q = 2 * (s % 2) + (par if rel == 0 else 1 - par)
        return xg.at[s // 2, zz, c, (y + dy) % 4, :, pl.ds(pl.multiple_of(q * 1024, 1024), 1024)]

    def group(dz, rel, s, cc):
        zz = zh if dz == 0 else 1 - zh
        q = 2 * (s % 2) + (par if rel == 0 else 1 - par)
        return xg.at[s // 2, zz, cc, :, :, pl.ds(pl.multiple_of(q * 1024, 1024), 1024)]

    DY = {"m": 3, "p": 1, "2": 2}

    def spread_y(dz, s):
        ref = piece(dz, 0, 0, s)
        send(ref, yp, ("y+", dz, s), ("y", dz, "m", s))
        send(ref, ym, ("y-", dz, s), ("y", dz, "p", s))

    def share_x(dz, who, s):
        ref = piece(dz, DY[who], 0, s)
        forward = {"m": True, "p": False, "2": s % 2 == 0}[who]
        forward = forward if s < 2 else not forward
        send(ref, xp if forward else xm, ("x+", dz, who, s), ("x", dz, who, s))

    def on_y(dz, who, s):
        landed(piece(dz, DY[who], 0, s), ("y", dz, who, s))
        if who == "m" and s % 2 == 0:
            send(piece(dz, DY[who], 0, s), yp, ("y2", dz, s), ("y", dz, "2", s))
        if who == "p" and s % 2 == 1:
            send(piece(dz, DY[who], 0, s), ym, ("y2", dz, s), ("y", dz, "2", s))
        share_x(dz, who, s)

    def on_x(dz, who, s):
        landed(piece(dz, DY[who], 1, s), ("x", dz, who, s))

    def at_edge(ref, to, name_here, name_there):
        cp = pltpu.make_async_remote_copy(
            ref, ref, send_sem[name_here], recv_sem[name_there], device_id=to, device_id_type=MESH)
        pl.when(edge)(cp.start)
        edge_pending.append(cp)

    edge_pending = []

    def on_z(rel, s):
        ref = piece(1, 0, rel, s)
        landed(ref, ("z", rel, s))
        at_edge(ref, inn, ("zi", rel, s), ("z", rel, s))
        if rel == 0:
            spread_y(1, s)

    def to_sibling(dz, rel, s):
        send(group(dz, rel, s, c), sib, ("c", dz, rel, s), ("c", dz, rel, s))

    started = set()

    def multiply(dz, rel, s):
        landed(group(dz, rel, s, 1 - c), ("c", dz, rel, s))
        zz = zh if dz == 0 else 1 - zh
        q = 2 * (s % 2) + (par if rel == 0 else 1 - par)
        cols = pl.ds(pl.multiple_of(q * 1024, 1024), 1024)
        arr = s // 2
        rows = xg[arr, zz, :, :, :, cols].reshape(256, 1024)
        w, acc, tiles = (wgu, accx, 3) if arr == 0 else (wd, accg, 3)
        size = 256 if arr == 0 else 128
        for m in range(tiles):
            at = pl.ds(m * size, size)
            value = lax.dot_general(w[at, cols], rows, NT, preferred_element_type=jnp.float32)
            if (dz, arr) in started:
                acc[dz, at, :] += value
            else:
                acc[dz, at, :] = value
        started.add((dz, arr))

    def lblock(dz, dy):
        return lmat.at[zh if dz == 0 else 1 - zh, c, (y + dy) % 4]

    def l_spread(dz):
        send(lblock(dz, 0), yp, ("ly+", dz), ("ly", dz, "m"))
        send(lblock(dz, 0), ym, ("ly-", dz), ("ly", dz, "p"))

    def l_on_y(dz):
        landed(lblock(dz, 3), ("ly", dz, "m"))
        send(lblock(dz, 3), yp, ("ly2", dz), ("ly", dz, "2"))
        landed(lblock(dz, 1), ("ly", dz, "p"))

    def l_sibling(dz):
        landed(lblock(dz, 2), ("ly", dz, "2"))
        zz = zh if dz == 0 else 1 - zh
        ref = lmat.at[zz, c]
        send(ref, sib, ("lc", dz), ("lc", dz))

    def l_done(dz):
        zz = zh if dz == 0 else 1 - zh
        landed(lmat.at[zz, 1 - c], ("lc", dz))

    for s in range(4):
        spread_y(0, s)
        at_edge(piece(0, 0, 0, s), outn, ("zo", 0, s), ("z", 0, s))
        if s == 0:
            l_spread(0)
            at_edge(lblock(0, 0), outn, ("lzo",), ("lz",))
    for s in range(4):
        at_edge(piece(0, 0, 1, s), outn, ("zo", 1, s), ("z", 1, s))
    w_gate.wait()
    w_up.wait()
    w_down.wait()
    l_on_y(0)
    for s in range(4):
        on_y(0, "m", s)
        on_y(0, "p", s)
        if s == 1:
            landed(lblock(1, 0), ("lz",))
            at_edge(lblock(1, 0), inn, ("lzi",), ("lz",))
            l_spread(1)
            l_sibling(0)
        if s >= 1:
            on_z(0, s - 1)
    on_z(0, 3)
    for s in range(4):
        landed(piece(0, 2, 0, s), ("y", 0, "2", s))
        share_x(0, "2", s)
        to_sibling(0, 0, s)
    l_on_y(1)
    for s in range(4):
        on_x(0, "m", s)
        on_x(0, "p", s)
    for s in range(2):
        on_y(1, "m", s)
        on_y(1, "p", s)
    l_sibling(1)
    multiply(0, 0, 0)
    for s in range(2):
        on_z(1, s)
        on_y(1, "m", s + 2)
        on_y(1, "p", s + 2)
    multiply(0, 0, 1)
    for s in range(4):
        on_x(0, "2", s)
        to_sibling(0, 1, s)
    on_z(1, 2)
    on_z(1, 3)
    multiply(0, 0, 2)
    multiply(0, 0, 3)

    l_done(0)
    l_done(1)
    half = lax.broadcasted_iota(jnp.int32, (8, 256), 0) < 4

    def over_experts(v, op, fold):
        t = op(v, axis=0)
        a = op(t[0:4], axis=0, keepdims=True)
        b = op(t[4:8], axis=0, keepdims=True)
        return jnp.where(half, a, b)

    for zz in range(2):
        flipped = lmat[zz].reshape(256, 128).T
        for k in range(16):
            probs[k, pl.ds(zz * 4, 4), :] = flipped[k * 4 : k * 4 + 4]
            chosen[k, pl.ds(zz * 4, 4), :] = flipped[64 + k * 4 : 68 + k * 4]
    raw = probs[...]
    raised = jnp.exp(raw - over_experts(raw, jnp.max, None))
    probs[...] = raised / over_experts(raised, jnp.sum, None)

    for s in range(4):
        landed(piece(1, 2, 0, s), ("y", 1, "2", s))
        share_x(1, "2", s)
        to_sibling(1, 0, s)
        multiply(0, 1, s)
    for s in range(4):
        on_x(1, "m", s)
        on_x(1, "p", s)
        on_x(1, "2", s)
        to_sibling(1, 1, s)
        multiply(1, 0, s)
    for s in range(4):
        multiply(1, 1, s)

    def local_scores(dz):
        g = accx[dz, 0:384, :]
        hidden = g / (1.0 + jnp.exp(-g)) * accx[dz, 384:768, :]
        both = hidden * accg[dz]
        return jnp.concatenate([jnp.sum(both[k * 96 : k * 96 + 96], axis=0, keepdims=True) for k in range(4)], axis=0)

    here, there = local_scores(0), local_scores(1)
    part[...] = jnp.where(zh == 0, jnp.concatenate([here, there], 0), jnp.concatenate([there, here], 0))

    sends = []
    for k in range(1, 16):
        to = (d + k) % 16
        cp = pltpu.make_async_remote_copy(
            part, got1.at[k], send_sem[("s1", k)], recv_sem[("s1", k)], device_id=(to, e), device_id_type=MESH)
        cp.start()
        sends.append(cp)
    total = part[...]
    for k in range(1, 16):
        sends[k - 1].wait_recv()
        total += got1[k]
    got2[e] = total
    sends2 = []
    for k in range(1, 16):
        to = (e + k) % 16
        mine = got2.at[e]
        cp = pltpu.make_async_remote_copy(
            mine, mine, send_sem[("s2", k)], recv_sem[("s2", k)], device_id=(d, to), device_id_type=MESH)
        cp.start()
        sends2.append(cp)
    for k in range(1, 16):
        theirs = got2.at[(e + 16 - k) % 16]
        pltpu.make_async_remote_copy(
            theirs, theirs, send_sem[("s2", k)], recv_sem[("s2", k)], device_id=sib, device_id_type=MESH).wait_recv()

    scores = got2[...]
    pr, ch = probs[...], chosen[...]
    kept = pr * ch
    mass = over_experts(kept, jnp.sum, None)
    weighted = over_experts(kept * scores, jnp.sum, None)
    prob_grad = scores / mass - ch * (weighted / (mass * mass))
    grad = pr * (prob_grad - over_experts(pr * prob_grad, jnp.sum, None))
    for k in range(16):
        lgc[0, pl.ds(k * 4, 4), :] = grad[k, 0:4]
        lgc[1, pl.ds(k * 4, 4), :] = grad[k, 4:8]
    turned[...] = lgc[zh].T
    lg_out[...] = turned[pl.ds(c * 128 + y * 32, 32), :]
    cols = pl.ds(pl.multiple_of(d * 256, 256), 256)
    rg = jnp.zeros((64, 256), jnp.float32)
    for zz in range(2):
        rows = xg[0, zz, :, :, :, cols].reshape(256, 256)
        rg += jnp.dot(lgc[zz].astype(jnp.bfloat16), rows, preferred_element_type=jnp.float32)
    rg_out[...] = rg.T

    for cp in pending + sends + sends2:
        cp.wait_send()

    @pl.when(edge)
    def _():
        for cp in edge_pending:
            cp.wait_send()


N_SEND, N_RECV = 160, 128


def per_device(tokens, cotangent, logits, routes, gate_weight, up_weight, down_weight):
    flat = [w.reshape(384, 4096) for w in (gate_weight, up_weight, down_weight)]
    hbm, vmem = pl.BlockSpec(memory_space=pl.ANY), pl.BlockSpec(memory_space=pltpu.VMEM)
    f32, bf16 = jnp.float32, jnp.bfloat16
    return pl.pallas_call(
        kernel,
        out_shape=(jax.ShapeDtypeStruct((32, 64), f32), jax.ShapeDtypeStruct((256, 64), f32)),
        in_specs=[hbm, hbm, vmem, vmem, hbm, hbm, hbm],
        out_specs=(vmem, vmem),
        scratch_shapes=[
            pltpu.VMEM((2, 2, 2, 4, 32, 4096), bf16),
            pltpu.VMEM((768, 4096), bf16),
            pltpu.VMEM((384, 4096), bf16),
            pltpu.VMEM((2, 768, 256), f32),
            pltpu.VMEM((2, 384, 256), f32),
            pltpu.VMEM((2, 2, 4, 32, 128), f32),
            pltpu.VMEM((16, 8, 256), f32),
            pltpu.VMEM((16, 8, 256), f32),
            pltpu.VMEM((8, 256), f32),
            pltpu.VMEM((16, 8, 256), f32),
            pltpu.VMEM((16, 8, 256), f32),
            pltpu.VMEM((2, 64, 256), f32),
            pltpu.VMEM((256, 64), f32),
            pltpu.SemaphoreType.DMA((5,)),
            pltpu.SemaphoreType.DMA((N_SEND,)),
            pltpu.SemaphoreType.DMA((N_RECV,)),
        ],
        compiler_params=pltpu.CompilerParams(
            collective_id=0, has_side_effects=True, vmem_limit_bytes=60 * MIB),
        cost_estimate=pl.CostEstimate(flops=2 * 512 * 384 * 4096 * 3, bytes_accessed=10 * MIB, transcendentals=512 * 384),
        name="router_grad",
    )(tokens, cotangent, logits, routes, *flat)


def solution(mesh):
    rows = P("dp", None)
    placed = (rows, rows, rows, rows) + (P("expert", "dp", None),) * 3
    return jax.shard_map(
        per_device, mesh=mesh, in_specs=placed, out_specs=(rows, rows), check_vma=False)
```

```python
import jax
import jax.numpy as jnp
from jax import lax
from jax.experimental import pallas as pl
from jax.experimental.pallas import tpu as pltpu
from jax.sharding import PartitionSpec as P

MESH = pl.DeviceIdType.MESH
MIB = 1024 * 1024
NT = (((1,), (1,)), ((), ()))


class Sems:
    def __init__(self, ref):
        self.ref, self.names = ref, {}

    def __getitem__(self, name):
        return self.ref.at[self.names.setdefault(name, len(self.names))]


def kernel(tok, cot, logits, routes, gate, up, down, lg_out, rg_out,
           xg, wgu, wd, accx, accg, lmat, probs, chosen, part, total, got_y, got_z, got2, lgc, turned,
           load_sem, send_ref, recv_ref, met):
    d = lax.axis_index("dp")
    e = lax.axis_index("expert")
    y, zh, c = d // 4, (d // 2) % 2, d % 2
    x, zl = e // 4, e % 4
    z = zh * 4 + zl
    par = x % 2
    send_sem, recv_sem = Sems(send_ref), Sems(recv_ref)

    def dev(x_, y_, z_, c_):
        return ((y_ * 2 + z_ // 4) * 2 + c_, x_ * 4 + z_ % 4)

    xp, xm = dev((x + 1) % 4, y, z, c), dev((x + 3) % 4, y, z, c)
    yp, ym = dev(x, (y + 1) % 4, z, c), dev(x, (y + 3) % 4, z, c)
    zp, zm = dev(x, y, (z + 1) % 8, c), dev(x, y, (z + 7) % 8, c)
    low = zl < 2
    outn = tuple(jnp.where(low, a, b) for a, b in zip(zm, zp))
    inn = tuple(jnp.where(low, a, b) for a, b in zip(zp, zm))
    sib = dev(x, y, z, 1 - c)
    edge = (zl == 0) | (zl == 3)

    own_x = pltpu.make_async_copy(tok, xg.at[0, zh, c, y], load_sem.at[0])
    own_g = pltpu.make_async_copy(cot, xg.at[1, zh, c, y], load_sem.at[1])
    w_gate = pltpu.make_async_copy(gate, wgu.at[pl.ds(0, 384)], load_sem.at[2])
    w_up = pltpu.make_async_copy(up, wgu.at[pl.ds(384, 384)], load_sem.at[3])
    w_down = pltpu.make_async_copy(down, wd, load_sem.at[4])
    barrier = pltpu.get_barrier_semaphore()
    for to in (yp, ym, xp, xm, zp, zm, sib):
        pl.semaphore_signal(barrier, inc=1, device_id=to, device_id_type=MESH)
    own_x.start()
    own_g.start()
    w_gate.start()
    w_up.start()
    w_down.start()
    expert = lax.broadcasted_iota(jnp.int32, (64, 32), 0)
    picked = jnp.zeros((64, 32), jnp.float32)
    for k in range(8):
        picked += (routes[k : k + 1, :] == expert).astype(jnp.float32)
    lmat[zh, c, y, :, pl.ds(0, 64)] = logits[...]
    lmat[zh, c, y, :, pl.ds(64, 64)] = picked.T
    own_x.wait()
    own_g.wait()
    pl.semaphore_wait(barrier, 7)

    pending = []

    def ship(ref, to, name_here, name_there):
        cp = pltpu.make_async_remote_copy(
            ref, ref, send_sem[name_here], recv_sem[name_there], device_id=to, device_id_type=MESH)
        cp.start()
        return cp

    def send(ref, to, name_here, name_there):
        pending.append(ship(ref, to, name_here, name_there))

    def landed(ref, name):
        pltpu.make_async_remote_copy(
            ref, ref, send_sem[("x+", 0, "m", 0)], recv_sem[name], device_id=sib, device_id_type=MESH).wait_recv()

    def piece(dz, dy, rel, s):
        zz = zh if dz == 0 else 1 - zh
        q = 2 * (s % 2) + (par if rel == 0 else 1 - par)
        return xg.at[s // 2, zz, c, (y + dy) % 4, :, pl.ds(pl.multiple_of(q * 1024, 1024), 1024)]

    def group(dz, rel, s, cc):
        zz = zh if dz == 0 else 1 - zh
        q = 2 * (s % 2) + (par if rel == 0 else 1 - par)
        return xg.at[s // 2, zz, cc, :, :, pl.ds(pl.multiple_of(q * 1024, 1024), 1024)]

    DY = {"m": 3, "p": 1, "2": 2}

    def spread_y(dz, s):
        ref = piece(dz, 0, 0, s)
        send(ref, yp, ("y+", dz, s), ("y", dz, "m", s))
        send(ref, ym, ("y-", dz, s), ("y", dz, "p", s))

    def share_x(dz, who, s):
        ref = piece(dz, DY[who], 0, s)
        forward = {"m": True, "p": False, "2": s % 2 == 0}[who]
        forward = forward if s < 2 else not forward
        send(ref, xp if forward else xm, ("x+", dz, who, s), ("x", dz, who, s))

    def on_y(dz, who, s):
        landed(piece(dz, DY[who], 0, s), ("y", dz, who, s))
        if who == "m" and s % 2 == 0:
            send(piece(dz, DY[who], 0, s), yp, ("y2", dz, s), ("y", dz, "2", s))
        if who == "p" and s % 2 == 1:
            send(piece(dz, DY[who], 0, s), ym, ("y2", dz, s), ("y", dz, "2", s))
        share_x(dz, who, s)

    def on_x(dz, who, s):
        landed(piece(dz, DY[who], 1, s), ("x", dz, who, s))

    edge_pending = []

    def at_edge(ref, to, name_here, name_there):
        cp = pltpu.make_async_remote_copy(
            ref, ref, send_sem[name_here], recv_sem[name_there], device_id=to, device_id_type=MESH)
        pl.when(edge)(cp.start)
        edge_pending.append(cp)

    def z_edge(rel, s):
        ref = piece(1, 0, rel, s)
        on = pltpu.make_async_remote_copy(
            ref, ref, send_sem[("zi", rel, s)], recv_sem[("z", rel, s)], device_id=inn, device_id_type=MESH)
        edge_pending.append(on)

        @pl.when(edge)
        def _():
            landed(ref, ("z", rel, s))
            on.start()

    def z_inner(rel, s):
        pl.when(~edge)(lambda: landed(piece(1, 0, rel, s), ("z", rel, s)))

    def to_sibling(dz, rel, s):
        send(group(dz, rel, s, c), sib, ("c", dz, rel, s), ("c", dz, rel, s))

    started = set()

    def multiply(dz, rel, s):
        landed(group(dz, rel, s, 1 - c), ("c", dz, rel, s))
        zz = zh if dz == 0 else 1 - zh
        q = 2 * (s % 2) + (par if rel == 0 else 1 - par)
        cols = pl.ds(pl.multiple_of(q * 1024, 1024), 1024)
        arr = s // 2
        rows = xg[arr, zz, :, :, :, cols].reshape(256, 1024)
        w, acc, tiles = (wgu, accx, (0, 256, 512)) if arr == 0 else (wd, accg, (0, 256))
        for m in tiles:
            at = pl.ds(m, min(256, w.shape[0] - m))
            value = lax.dot_general(w[at, cols], rows, NT, preferred_element_type=jnp.float32)
            if (dz, arr) in started:
                acc[dz, at, :] += value
            else:
                acc[dz, at, :] = value
        started.add((dz, arr))

    def lblock(dz, dy):
        return lmat.at[zh if dz == 0 else 1 - zh, c, (y + dy) % 4]

    def l_spread(dz):
        send(lblock(dz, 0), yp, ("ly+", dz), ("ly", dz, "m"))
        send(lblock(dz, 0), ym, ("ly-", dz), ("ly", dz, "p"))

    def l_on_y(dz):
        landed(lblock(dz, 3), ("ly", dz, "m"))
        send(lblock(dz, 3), yp, ("ly2", dz), ("ly", dz, "2"))
        landed(lblock(dz, 1), ("ly", dz, "p"))

    def l_sibling(dz):
        landed(lblock(dz, 2), ("ly", dz, "2"))
        zz = zh if dz == 0 else 1 - zh
        ref = lmat.at[zz, c]
        send(ref, sib, ("lc", dz), ("lc", dz))

    def l_done(dz):
        zz = zh if dz == 0 else 1 - zh
        landed(lmat.at[zz, 1 - c], ("lc", dz))

    def greet(k):
        pl.semaphore_signal(met.at[2 * k], inc=1, device_id=zp, device_id_type=MESH)
        pl.semaphore_signal(met.at[2 * k + 1], inc=1, device_id=zm, device_id_type=MESH)

    def greeted(k):
        pl.semaphore_wait(met.at[2 * k], 1)
        pl.semaphore_wait(met.at[2 * k + 1], 1)

    def on_y_both(dz, s):
        on_y(dz, "m", s)
        on_y(dz, "p", s)

    def on_y2(dz, s):
        landed(piece(dz, 2, 0, s), ("y", dz, "2", s))
        share_x(dz, "2", s)
        to_sibling(dz, 0, s)

    def on_x_all(dz, s):
        on_x(dz, "m", s)
        on_x(dz, "p", s)
        on_x(dz, "2", s)
        to_sibling(dz, 1, s)

    def l_edge():
        on = pltpu.make_async_remote_copy(
            lblock(1, 0), lblock(1, 0), send_sem[("lzi",)], recv_sem[("lz",)], device_id=inn, device_id_type=MESH)
        edge_pending.append(on)

        @pl.when(edge)
        def _():
            landed(lblock(1, 0), ("lz",))
            on.start()

    def l_on_z():
        pl.when(~edge)(lambda: landed(lblock(1, 0), ("lz",)))
        l_spread(1)

    l_spread(0)
    at_edge(lblock(0, 0), outn, ("lzo",), ("lz",))
    for s in range(4):
        spread_y(0, s)
        at_edge(piece(0, 0, 0, s), outn, ("zo", 0, s), ("z", 0, s))
    for s in range(4):
        at_edge(piece(0, 0, 1, s), outn, ("zo", 1, s), ("z", 1, s))
    greet(0)
    w_gate.wait()
    w_up.wait()
    w_down.wait()
    on_y_both(0, 0)
    l_edge()
    z_edge(0, 0)
    on_y_both(0, 1)
    z_edge(0, 1)
    l_on_y(0)
    greeted(0)
    greet(1)
    on_y_both(0, 2)
    z_edge(0, 2)
    z_inner(0, 0)
    spread_y(1, 0)
    on_y_both(0, 3)
    z_edge(0, 3)
    z_inner(0, 1)
    spread_y(1, 1)
    on_y2(0, 0)
    z_edge(1, 0)
    greeted(1)
    greet(2)
    on_y2(0, 1)
    z_inner(0, 2)
    spread_y(1, 2)
    z_edge(1, 1)
    on_y2(0, 2)
    z_inner(0, 3)
    spread_y(1, 3)
    z_edge(1, 2)
    l_on_z()
    multiply(0, 0, 0)
    on_y2(0, 3)
    z_edge(1, 3)
    multiply(0, 0, 1)
    l_sibling(0)
    on_y_both(1, 0)
    multiply(0, 0, 2)
    on_y_both(1, 1)
    multiply(0, 0, 3)
    on_x_all(0, 0)
    on_y_both(1, 2)
    l_on_y(1)
    on_x_all(0, 1)
    multiply(0, 1, 0)
    on_y_both(1, 3)
    on_x_all(0, 2)
    multiply(0, 1, 1)
    on_y2(1, 0)
    on_x_all(0, 3)
    multiply(0, 1, 2)
    on_y2(1, 1)
    multiply(0, 1, 3)
    z_inner(1, 0)
    z_inner(1, 1)
    on_y2(1, 2)
    multiply(1, 0, 0)
    z_inner(1, 2)
    z_inner(1, 3)
    greeted(2)
    on_y2(1, 3)
    l_sibling(1)
    multiply(1, 0, 1)
    on_x_all(1, 0)
    multiply(1, 0, 2)

    l_done(0)
    l_done(1)
    half = lax.broadcasted_iota(jnp.int32, (8, 256), 0) < 4

    def over_experts(v, op):
        t = op(v, axis=0)
        a = op(t[0:4], axis=0, keepdims=True)
        b = op(t[4:8], axis=0, keepdims=True)
        return jnp.where(half, a, b)

    for zz in range(2):
        flipped = lmat[zz].reshape(256, 128).T
        for k in range(16):
            probs[k, pl.ds(zz * 4, 4), :] = flipped[k * 4 : k * 4 + 4]
            chosen[k, pl.ds(zz * 4, 4), :] = flipped[64 + k * 4 : 68 + k * 4]
    raw = probs[...]
    raised = jnp.exp(raw - over_experts(raw, jnp.max))
    probs[...] = raised / over_experts(raised, jnp.sum)

    on_x_all(1, 1)
    multiply(1, 0, 3)
    on_x_all(1, 2)
    multiply(1, 1, 0)
    on_x_all(1, 3)
    multiply(1, 1, 1)
    multiply(1, 1, 2)
    multiply(1, 1, 3)

    def local_scores(dz):
        g = accx[dz, 0:384, :]
        hidden = g / (1.0 + jnp.exp(-g)) * accx[dz, 384:768, :]
        both = hidden * accg[dz]
        return jnp.concatenate([jnp.sum(both[k * 96 : k * 96 + 96], axis=0, keepdims=True) for k in range(4)], axis=0)

    here, there = local_scores(0), local_scores(1)
    part[...] = jnp.where(zh == 0, jnp.concatenate([here, there], 0), jnp.concatenate([there, here], 0))

    def exchange(tag, source, place, peers):
        copies = {}
        for k, to in peers:
            copies[k] = pltpu.make_async_remote_copy(
                source, place(k), send_sem[(tag, k)], recv_sem[(tag, k)], device_id=to, device_id_type=MESH)
            copies[k].start()
        pending.extend(copies.values())
        return copies

    copies = exchange("ty", part, lambda k: got_y.at[k], [
        (dy * 2 + dc, dev(x, (y + dy) % 4, z, (c + dc) % 2)) for dy, dc in ((2, 1), (2, 0), (1, 1), (3, 1), (1, 0), (3, 0), (0, 1))])
    for k in (1, 2, 6, 3, 7, 4, 5):
        copies[k].wait_recv()
    total[...] = part[...] + sum(got_y[k] for k in range(1, 8))
    copies = exchange("tz", total, lambda k: got_z.at[k], [(k, dev(x, y, (z + k) % 8, c)) for k in (4, 3, 5, 2, 6, 1, 7)])
    for k in (1, 7, 2, 6, 3, 5, 4):
        copies[k].wait_recv()
    for k in range(4):
        first = total[...] if k == 0 else got_z[k]
        got2[x * 4 + (z + 8 - k) % 4] = first + got_z[k + 4]
    mine = got2.at[pl.ds(x * 4, 4)]
    copies = exchange("tx", mine, lambda k: mine, [(k, dev((x + k) % 4, y, z, c)) for k in (2, 1, 3)])
    for k in (1, 3, 2):
        theirs = got2.at[pl.ds((x + 4 - k) % 4 * 4, 4)]
        pltpu.make_async_remote_copy(
            theirs, theirs, send_sem[("tx", k)], recv_sem[("tx", k)], device_id=sib, device_id_type=MESH).wait_recv()

    scores = got2[...]
    pr, ch = probs[...], chosen[...]
    kept = pr * ch
    mass = over_experts(kept, jnp.sum)
    weighted = over_experts(kept * scores, jnp.sum)
    prob_grad = scores / mass - ch * (weighted / (mass * mass))
    grad = pr * (prob_grad - over_experts(pr * prob_grad, jnp.sum))
    for k in range(16):
        lgc[0, pl.ds(k * 4, 4), :] = grad[k, 0:4]
        lgc[1, pl.ds(k * 4, 4), :] = grad[k, 4:8]
    turned[...] = lgc[zh].T
    lg_out[...] = turned[pl.ds(c * 128 + y * 32, 32), :]
    cols = pl.ds(pl.multiple_of(d * 256, 256), 256)
    rg = jnp.zeros((64, 256), jnp.float32)
    for zz in range(2):
        rows = xg[0, zz, :, :, :, cols].reshape(256, 256)
        rg += jnp.dot(lgc[zz].astype(jnp.bfloat16), rows, preferred_element_type=jnp.float32)
    rg_out[...] = rg

    for cp in pending:
        cp.wait_send()

    @pl.when(edge)
    def _():
        for cp in edge_pending:
            cp.wait_send()


N_SEND, N_RECV = 160, 128


def per_device(tokens, cotangent, logits, routes, gate_weight, up_weight, down_weight):
    flat = [w.reshape(384, 4096) for w in (gate_weight, up_weight, down_weight)]
    hbm, vmem = pl.BlockSpec(memory_space=pl.ANY), pl.BlockSpec(memory_space=pltpu.VMEM)
    f32, bf16 = jnp.float32, jnp.bfloat16
    logit_grad, router_grad = pl.pallas_call(
        kernel,
        out_shape=(jax.ShapeDtypeStruct((32, 64), f32), jax.ShapeDtypeStruct((64, 256), f32)),
        in_specs=[hbm, hbm, vmem, vmem, hbm, hbm, hbm],
        out_specs=(vmem, vmem),
        scratch_shapes=[
            pltpu.VMEM((2, 2, 2, 4, 32, 4096), bf16),
            pltpu.VMEM((768, 4096), bf16),
            pltpu.VMEM((384, 4096), bf16),
            pltpu.VMEM((2, 768, 256), f32),
            pltpu.VMEM((2, 384, 256), f32),
            pltpu.VMEM((2, 2, 4, 32, 128), f32),
            pltpu.VMEM((16, 8, 256), f32),
            pltpu.VMEM((16, 8, 256), f32),
            pltpu.VMEM((8, 256), f32),
            pltpu.VMEM((8, 256), f32),
            pltpu.VMEM((8, 8, 256), f32),
            pltpu.VMEM((8, 8, 256), f32),
            pltpu.VMEM((16, 8, 256), f32),
            pltpu.VMEM((2, 64, 256), f32),
            pltpu.VMEM((256, 64), f32),
            pltpu.SemaphoreType.DMA((5,)),
            pltpu.SemaphoreType.DMA((N_SEND,)),
            pltpu.SemaphoreType.DMA((N_RECV,)),
            pltpu.SemaphoreType.REGULAR((6,)),
        ],
        compiler_params=pltpu.CompilerParams(
            collective_id=0, has_side_effects=True, vmem_limit_bytes=60 * MIB),
        cost_estimate=pl.CostEstimate(flops=2 * 512 * 384 * 4096 * 3, bytes_accessed=10 * MIB, transcendentals=512 * 384),
        name="router_grad",
    )(tokens, cotangent, logits, routes.T, *flat)
    return logit_grad, router_grad.T


def solution(mesh):
    rows = P("dp", None)
    placed = (rows, rows, rows, rows) + (P("expert", "dp", None),) * 3
    return jax.shard_map(
        per_device, mesh=mesh, in_specs=placed, out_specs=(rows, rows), check_vma=False)
```

```python
import jax
import jax.numpy as jnp
from jax import lax
from jax.experimental import pallas as pl
from jax.experimental.pallas import tpu as pltpu
from jax.sharding import PartitionSpec as P

MESH = pl.DeviceIdType.MESH
MIB = 1024 * 1024
NT = (((1,), (1,)), ((), ()))


class Sems:
    def __init__(self, ref):
        self.ref, self.names = ref, {}

    def __getitem__(self, name):
        return self.ref.at[self.names.setdefault(name, len(self.names))]


def kernel(tok, cot, logits, routes, gate, up, down, lg_out, rg_out,
           xg, wgu, wd, accx, accg, lmat, probs, chosen, part, total, got_y, got_z, got2, lgc, turned,
           load_sem, send_ref, recv_ref, out_sem, in_sem, met):
    d = lax.axis_index("dp")
    e = lax.axis_index("expert")
    y, zh, c = d // 4, (d // 2) % 2, d % 2
    x, zl = e // 4, e % 4
    z = zh * 4 + zl
    par = x % 2
    send_sem, recv_sem = Sems(send_ref), Sems(recv_ref)

    def dev(x_, y_, z_, c_):
        return ((y_ * 2 + z_ // 4) * 2 + c_, x_ * 4 + z_ % 4)

    xp, xm = dev((x + 1) % 4, y, z, c), dev((x + 3) % 4, y, z, c)
    yp, ym = dev(x, (y + 1) % 4, z, c), dev(x, (y + 3) % 4, z, c)
    zp, zm = dev(x, y, (z + 1) % 8, c), dev(x, y, (z + 7) % 8, c)
    low = zl < 2
    outn = tuple(jnp.where(low, a, b) for a, b in zip(zm, zp))
    inn = tuple(jnp.where(low, a, b) for a, b in zip(zp, zm))
    sib = dev(x, y, z, 1 - c)
    edge = (zl == 0) | (zl == 3)

    barrier = pltpu.get_barrier_semaphore()
    for to in (yp, ym, xp, xm, zp, zm, sib):
        pl.semaphore_signal(barrier, inc=1, device_id=to, device_id_type=MESH)
    own_x = pltpu.make_async_copy(tok, xg.at[0, zh, c, y], load_sem.at[0])
    own_g = pltpu.make_async_copy(cot, xg.at[1, zh, c, y], load_sem.at[1])
    w_gate = pltpu.make_async_copy(gate, wgu.at[pl.ds(0, 384)], load_sem.at[2])
    w_up = pltpu.make_async_copy(up, wgu.at[pl.ds(384, 384)], load_sem.at[3])
    w_down = pltpu.make_async_copy(down, wd, load_sem.at[4])

    pending, final = [], []

    def send(like, to, name_here, name_there, source=None):
        ref = like()
        cp = pltpu.make_async_remote_copy(
            ref if source is None else source, ref, send_sem[name_here], recv_sem[name_there],
            device_id=to, device_id_type=MESH)
        cp.start()
        pending.append((name_here, like))

    def landed(ref, name):
        pltpu.make_async_remote_copy(
            ref, ref, send_sem[("x+", 0, "m", 0)], recv_sem[name], device_id=sib, device_id_type=MESH).wait_recv()

    def eighth(rel, s):
        q = 2 * (s // 2 % 2) + (par if rel == 0 else 1 - par)
        return pl.ds(pl.multiple_of(q * 1024 + s % 2 * 512, 512), 512)

    def piece(dz, dy, rel, s):
        zz = zh if dz == 0 else 1 - zh
        return xg.at[s // 4, zz, c, (y + dy) % 4, :, eighth(rel, s)]

    def group(dz, rel, s, cc):
        zz = zh if dz == 0 else 1 - zh
        q = 2 * (s % 2) + (par if rel == 0 else 1 - par)
        return xg.at[s // 2, zz, cc, :, :, pl.ds(pl.multiple_of(q * 1024, 1024), 1024)]

    DY = {"m": 3, "p": 1, "2": 2}

    def given(rel, s):
        return (tok, cot)[s // 4].at[:, eighth(rel, s)]

    def spread_y(dz, s):
        source = given(0, s) if dz == 0 else None
        send(lambda: piece(dz, 0, 0, s), yp, ("y+", dz, s), ("y", dz, "m", s), source)
        send(lambda: piece(dz, 0, 0, s), ym, ("y-", dz, s), ("y", dz, "p", s), source)

    def share_x(dz, who, s):
        forward = {"m": True, "p": False, "2": s % 2 == 0}[who]
        forward = forward if s < 4 else not forward
        send(lambda: piece(dz, DY[who], 0, s), xp if forward else xm, ("x+", dz, who, s), ("x", dz, who, s))

    def on_y(dz, who, s):
        landed(piece(dz, DY[who], 0, s), ("y", dz, who, s))
        if who == "m" and s % 2 == 0:
            send(lambda: piece(dz, DY[who], 0, s), yp, ("y2", dz, s), ("y", dz, "2", s))
        if who == "p" and s % 2 == 1:
            send(lambda: piece(dz, DY[who], 0, s), ym, ("y2", dz, s), ("y", dz, "2", s))
        share_x(dz, who, s)

    def on_x(dz, who, s):
        landed(piece(dz, DY[who], 1, s), ("x", dz, who, s))

    edge_pending = []

    def at_edge(like, to, name_here, name_there, source=None, arrived=None):
        edge_pending.append((name_here, like))

        @pl.when(edge)
        def _():
            if arrived is not None:
                landed(like(), arrived)
            pltpu.make_async_remote_copy(
                like() if source is None else source, like(), send_sem[name_here], recv_sem[name_there],
                device_id=to, device_id_type=MESH).start()

    def z_edge(rel, quarter):
        for s in (2 * quarter, 2 * quarter + 1):
            at_edge(lambda s=s: piece(1, 0, rel, s), inn, ("zi", rel, s), ("z", rel, s), arrived=("z", rel, s))

    def z_in(rel, s):
        pl.when(~edge)(lambda: landed(piece(1, 0, rel, s), ("z", rel, s)))

    def z_inner(rel, quarter):
        for s in (2 * quarter, 2 * quarter + 1):
            z_in(rel, s)

    def to_sibling(dz, rel, s):
        k = dz * 8 + rel * 4 + s
        cp = pltpu.make_async_remote_copy(
            group(dz, rel, s, c), group(dz, rel, s, c), out_sem.at[k], in_sem.at[k], device_id=sib, device_id_type=MESH)
        cp.start()

    def multiply(step):
        dz, rel, s = step // 8, step // 4 % 2, step % 4
        zz = jnp.where(dz == 0, zh, 1 - zh)
        q = 2 * (s % 2) + jnp.where(rel == 0, par, 1 - par)
        cols = pl.ds(pl.multiple_of(q * 1024, 1024), 1024)
        arrived = xg.at[s // 2, zz, 1 - c, :, :, cols]
        pltpu.make_async_remote_copy(
            arrived, arrived, out_sem.at[step], in_sem.at[step], device_id=sib, device_id_type=MESH).wait_recv()

        def add(arr, w, acc):
            rows = xg[arr, zz, :, :, :, cols].reshape(256, 1024)
            size = 256 if arr == 0 else 384
            for m in range(0, w.shape[0], size):
                at = pl.ds(m, size)
                acc[dz, at, :] += lax.dot_general(w[at, cols], rows, NT, preferred_element_type=jnp.float32)

        pl.when(s < 2)(lambda: add(0, wgu, accx))
        pl.when(s >= 2)(lambda: add(1, wd, accg))

    def lblock(dz, dy):
        return lmat.at[zh if dz == 0 else 1 - zh, c, (y + dy) % 4]

    def l_spread(dz):
        send(lambda: lblock(dz, 0), yp, ("ly+", dz), ("ly", dz, "m"))
        send(lambda: lblock(dz, 0), ym, ("ly-", dz), ("ly", dz, "p"))

    def l_on_y(dz):
        landed(lblock(dz, 3), ("ly", dz, "m"))
        send(lambda: lblock(dz, 3), yp, ("ly2", dz), ("ly", dz, "2"))
        landed(lblock(dz, 1), ("ly", dz, "p"))

    def lgroup(dz, cc):
        return lmat.at[zh if dz == 0 else 1 - zh, cc]

    def l_sibling(dz):
        landed(lblock(dz, 2), ("ly", dz, "2"))
        send(lambda: lgroup(dz, c), sib, ("lc", dz), ("lc", dz))

    def l_done(dz):
        landed(lgroup(dz, 1 - c), ("lc", dz))

    def greet(k):
        pl.semaphore_signal(met.at[2 * k], inc=1, device_id=zp, device_id_type=MESH)
        pl.semaphore_signal(met.at[2 * k + 1], inc=1, device_id=zm, device_id_type=MESH)

    def greeted(k):
        pl.semaphore_wait(met.at[2 * k], 1)
        pl.semaphore_wait(met.at[2 * k + 1], 1)

    def halves(quarter):
        return (2 * quarter, 2 * quarter + 1)

    def on_y_both(dz, quarter):
        for s in halves(quarter):
            on_y(dz, "m", s)
            on_y(dz, "p", s)

    def on_y2(dz, quarter):
        for s in halves(quarter):
            landed(piece(dz, 2, 0, s), ("y", dz, "2", s))
            share_x(dz, "2", s)
        to_sibling(dz, 0, quarter)

    def on_x_all(dz, quarter):
        for s in halves(quarter):
            on_x(dz, "m", s)
            on_x(dz, "p", s)
            on_x(dz, "2", s)
        to_sibling(dz, 1, quarter)

    def l_edge():
        at_edge(lambda: lblock(1, 0), inn, ("lzi",), ("lz",), arrived=("lz",))

    def l_on_z():
        pl.when(~edge)(lambda: landed(lblock(1, 0), ("lz",)))
        l_spread(1)

    def own(quarter):
        for s in halves(quarter):
            spread_y(0, s)
            at_edge(lambda s=s: piece(0, 0, 0, s), outn, ("zo", 0, s), ("z", 0, s), given(0, s))

    def own_rest(quarter):
        for s in halves(quarter):
            at_edge(lambda s=s: piece(0, 0, 1, s), outn, ("zo", 1, s), ("z", 1, s), given(1, s))

    def other(quarter):
        for s in halves(quarter):
            z_in(0, s)
            spread_y(1, s)

    half = lax.broadcasted_iota(jnp.int32, (8, 256), 0) < 4

    def over_experts(v, op):
        t = op(v, axis=0)
        a = op(t[0:4], axis=0, keepdims=True)
        b = op(t[4:8], axis=0, keepdims=True)
        return jnp.where(half, a, b)

    def softmax():
        l_done(0)
        l_done(1)
        for zz in range(2):
            flipped = lmat[zz].reshape(256, 128).T
            for k in range(16):
                probs[k, pl.ds(zz * 4, 4), :] = flipped[k * 4 : k * 4 + 4]
                chosen[k, pl.ds(zz * 4, 4), :] = flipped[64 + k * 4 : 68 + k * 4]
        raw = probs[...]
        raised = jnp.exp(raw - over_experts(raw, jnp.max))
        probs[...] = raised / over_experts(raised, jnp.sum)

    expert = lax.broadcasted_iota(jnp.int32, (64, 32), 0)
    picked = jnp.zeros((64, 32), jnp.float32)
    for k in range(8):
        picked += (routes[k : k + 1, :] == expert).astype(jnp.float32)
    lmat[zh, c, y, :, pl.ds(0, 64)] = logits[...]
    lmat[zh, c, y, :, pl.ds(64, 64)] = picked.T
    pl.semaphore_wait(barrier, 7)
    own(0)
    l_spread(0)
    at_edge(lambda: lblock(0, 0), outn, ("lzo",), ("lz",))
    for s in range(1, 4):
        own(s)
    for s in range(4):
        own_rest(s)
    for cp in (own_x, own_g, w_gate, w_up, w_down):
        cp.start()
    greet(0)
    accx[...] = jnp.zeros_like(accx)
    accg[...] = jnp.zeros_like(accg)
    own_x.wait()
    own_g.wait()
    on_y_both(0, 0)
    l_edge()
    z_edge(0, 0)
    on_y_both(0, 1)
    z_edge(0, 1)
    l_on_y(0)
    greeted(0)
    greet(1)
    on_y_both(0, 2)
    z_edge(0, 2)
    other(0)
    l_on_z()
    on_y_both(0, 3)
    z_edge(0, 3)
    other(1)
    on_y2(0, 0)
    greeted(1)
    greet(2)
    on_y2(0, 1)
    other(2)
    z_edge(1, 0)
    on_y_both(1, 0)
    on_y2(0, 2)
    other(3)
    z_edge(1, 1)
    w_gate.wait()
    w_up.wait()
    w_down.wait()

    def before_1():
        on_y_both(1, 1)
        on_y2(0, 3)
        z_edge(1, 2)
        l_sibling(0)
        on_x_all(0, 0)

    def before_2():
        on_y_both(1, 2)
        z_edge(1, 3)
        on_x_all(0, 1)

    def before_3():
        on_y_both(1, 3)
        on_x_all(0, 2)

    def before_4():
        on_y2(1, 0)

    def before_5():
        on_y2(1, 1)
        l_on_y(1)
        greeted(2)

    def before_6():
        on_x_all(0, 3)

    def before_7():
        on_y2(1, 2)

    def before_8():
        on_y2(1, 3)
        z_inner(1, 0)
        on_x_all(1, 0)

    def before_9():
        l_sibling(1)
        z_inner(1, 1)
        on_x_all(1, 1)

    def before_11():
        z_inner(1, 2)
        on_x_all(1, 2)

    def before_13():
        z_inner(1, 3)
        on_x_all(1, 3)

    before = {1: before_1, 2: before_2, 3: before_3, 4: before_4, 5: before_5, 6: before_6, 7: before_7, 8: before_8,
              9: before_9, 11: before_11, 13: before_13, 14: softmax}

    def at_step(step, low, high):
        if not any(low <= k < high for k in before):
            return
        if high - low == 1:
            before[low]()
            return
        mid = (low + high) // 2
        lax.cond(step < mid, lambda: at_step(step, low, mid), lambda: at_step(step, mid, high))

    @pl.loop(0, 16)
    def _(step):
        at_step(step, 0, 16)
        multiply(step)

    def local_scores(dz):
        g = accx[dz, 0:384, :]
        hidden = g / (1.0 + jnp.exp(-g)) * accx[dz, 384:768, :]
        both = hidden * accg[dz]
        return jnp.concatenate([jnp.sum(both[k * 96 : k * 96 + 96], axis=0, keepdims=True) for k in range(4)], axis=0)

    here, there = local_scores(0), local_scores(1)
    part[...] = jnp.where(zh == 0, jnp.concatenate([here, there], 0), jnp.concatenate([there, here], 0))

    def exchange(tag, source, place, peers):
        copies = {}
        for k, to in peers:
            copies[k] = pltpu.make_async_remote_copy(
                source, place(k), send_sem[(tag, k)], recv_sem[(tag, k)], device_id=to, device_id_type=MESH)
            copies[k].start()
        final.extend(copies.values())
        return copies

    copies = exchange("ty", part, lambda k: got_y.at[k], [
        (dy * 2 + dc, dev(x, (y + dy) % 4, z, (c + dc) % 2)) for dy, dc in ((2, 1), (2, 0), (1, 1), (3, 1), (1, 0), (3, 0), (0, 1))])
    for k in (1, 2, 6, 3, 7, 4, 5):
        copies[k].wait_recv()
    total[...] = part[...] + sum(got_y[k] for k in range(1, 8))
    copies = exchange("tz", total, lambda k: got_z.at[k], [(k, dev(x, y, (z + k) % 8, c)) for k in (4, 3, 5, 2, 6, 1, 7)])
    for k in (1, 7, 2, 6, 3, 5, 4):
        copies[k].wait_recv()
    for k in range(4):
        first = total[...] if k == 0 else got_z[k]
        got2[x * 4 + (z + 8 - k) % 4] = first + got_z[k + 4]
    mine = got2.at[pl.ds(x * 4, 4)]
    copies = exchange("tx", mine, lambda k: mine, [(k, dev((x + k) % 4, y, z, c)) for k in (2, 1, 3)])
    for k in (1, 3, 2):
        theirs = got2.at[pl.ds((x + 4 - k) % 4 * 4, 4)]
        pltpu.make_async_remote_copy(
            theirs, theirs, send_sem[("tx", k)], recv_sem[("tx", k)], device_id=sib, device_id_type=MESH).wait_recv()

    scores = got2[...]
    pr, ch = probs[...], chosen[...]
    kept = pr * ch
    mass = over_experts(kept, jnp.sum)
    weighted = over_experts(kept * scores, jnp.sum)
    prob_grad = scores / mass - ch * (weighted / (mass * mass))
    grad = pr * (prob_grad - over_experts(pr * prob_grad, jnp.sum))
    for k in range(16):
        lgc[0, pl.ds(k * 4, 4), :] = grad[k, 0:4]
        lgc[1, pl.ds(k * 4, 4), :] = grad[k, 4:8]
    turned[...] = lgc[zh].T
    lg_out[...] = turned[pl.ds(c * 128 + y * 32, 32), :]
    cols = pl.ds(pl.multiple_of(d * 256, 256), 256)
    rg = jnp.zeros((64, 256), jnp.float32)
    for zz in range(2):
        rows = xg[0, zz, :, :, :, cols].reshape(256, 256)
        rg += jnp.dot(lgc[zz].astype(jnp.bfloat16), rows, preferred_element_type=jnp.float32)
    rg_out[...] = rg

    def sent(name, like):
        pltpu.make_async_remote_copy(
            like(), like(), send_sem[name], recv_sem[("lz",)], device_id=sib, device_id_type=MESH).wait_send()

    for name, like in pending:
        sent(name, like)
    for step in range(16):
        ref = group(0, 0, 0, c)
        pltpu.make_async_remote_copy(
            ref, ref, out_sem.at[step], in_sem.at[step], device_id=sib, device_id_type=MESH).wait_send()
    for cp in final:
        cp.wait_send()

    @pl.when(edge)
    def _():
        for name, like in edge_pending:
            sent(name, like)


N_SEND, N_RECV = 160, 160


def finish(lg, rg, lg_out, rg_out):
    lg_out[...] = lg[...]
    rg_out[...] = rg[...]


def per_device(tokens, cotangent, logits, routes, gate_weight, up_weight, down_weight):
    flat = [w.reshape(384, 4096) for w in (gate_weight, up_weight, down_weight)]
    hbm, vmem = pl.BlockSpec(memory_space=pl.ANY), pl.BlockSpec(memory_space=pltpu.VMEM)
    f32, bf16 = jnp.float32, jnp.bfloat16
    logit_grad, router_grad = pl.pallas_call(
        kernel,
        out_shape=(jax.ShapeDtypeStruct((32, 64), f32), jax.ShapeDtypeStruct((64, 256), f32)),
        in_specs=[hbm, hbm, vmem, vmem, hbm, hbm, hbm],
        out_specs=(vmem, vmem),
        scratch_shapes=[
            pltpu.VMEM((2, 2, 2, 4, 32, 4096), bf16),
            pltpu.VMEM((768, 4096), bf16),
            pltpu.VMEM((384, 4096), bf16),
            pltpu.VMEM((2, 768, 256), f32),
            pltpu.VMEM((2, 384, 256), f32),
            pltpu.VMEM((2, 2, 4, 32, 128), f32),
            pltpu.VMEM((16, 8, 256), f32),
            pltpu.VMEM((16, 8, 256), f32),
            pltpu.VMEM((8, 256), f32),
            pltpu.VMEM((8, 256), f32),
            pltpu.VMEM((8, 8, 256), f32),
            pltpu.VMEM((8, 8, 256), f32),
            pltpu.VMEM((16, 8, 256), f32),
            pltpu.VMEM((2, 64, 256), f32),
            pltpu.VMEM((256, 64), f32),
            pltpu.SemaphoreType.DMA((5,)),
            pltpu.SemaphoreType.DMA((N_SEND,)),
            pltpu.SemaphoreType.DMA((N_RECV,)),
            pltpu.SemaphoreType.DMA((16,)),
            pltpu.SemaphoreType.DMA((16,)),
            pltpu.SemaphoreType.REGULAR((6,)),
        ],
        compiler_params=pltpu.CompilerParams(
            collective_id=0, has_side_effects=True, vmem_limit_bytes=60 * MIB),
        cost_estimate=pl.CostEstimate(flops=2 * 512 * 384 * 4096 * 3, bytes_accessed=10 * MIB, transcendentals=512 * 384),
        name="router_grad",
    )(tokens, cotangent, logits, routes.T, *flat)
    logit_grad, router_grad = pl.pallas_call(
        finish,
        out_shape=(jax.ShapeDtypeStruct((32, 64), f32), jax.ShapeDtypeStruct((64, 256), f32)),
        in_specs=[vmem, vmem],
        out_specs=(vmem, vmem),
        name="finish",
    )(logit_grad, router_grad)
    return logit_grad, router_grad.T


def solution(mesh):
    rows = P("dp", None)
    placed = (rows, rows, rows, rows) + (P("expert", "dp", None),) * 3
    return jax.shard_map(
        per_device, mesh=mesh, in_specs=placed, out_specs=(rows, rows), check_vma=False)
```

```python
import jax
import jax.numpy as jnp
from jax import lax
from jax.experimental import pallas as pl
from jax.experimental.pallas import tpu as pltpu
from jax.sharding import PartitionSpec as P

MESH = pl.DeviceIdType.MESH
MIB = 1024 * 1024
NT = (((1,), (1,)), ((), ()))


class Sems:
    def __init__(self, ref):
        self.ref, self.names = ref, {}

    def __getitem__(self, name):
        k = self.names.setdefault(name, len(self.names))
        assert k < N_RECV
        return self.ref.at[k]


def kernel(tok, cot, logits, routes, gate, up, down, lg_out, rg_out,
           xg, wgu, wd, accx, accg, lmat, probs, chosen, part, total, got_y, got_z, got2, lgc, turned,
           load_sem, sent_sem, recv_ref, in_sem, met):
    d = lax.axis_index("dp")
    e = lax.axis_index("expert")
    y, zh, c = d // 4, (d // 2) % 2, d % 2
    x, zl = e // 4, e % 4
    z = zh * 4 + zl
    par = x % 2
    recv_sem = Sems(recv_ref)

    def dev(x_, y_, z_, c_):
        return ((y_ * 2 + z_ // 4) * 2 + c_, x_ * 4 + z_ % 4)

    xp, xm = dev((x + 1) % 4, y, z, c), dev((x + 3) % 4, y, z, c)
    yp, ym = dev(x, (y + 1) % 4, z, c), dev(x, (y + 3) % 4, z, c)
    zp, zm = dev(x, y, (z + 1) % 8, c), dev(x, y, (z + 7) % 8, c)
    low = zl < 2
    outn = tuple(jnp.where(low, a, b) for a, b in zip(zm, zp))
    inn = tuple(jnp.where(low, a, b) for a, b in zip(zp, zm))
    sib = dev(x, y, z, 1 - c)
    edge = (zl == 0) | (zl == 3)

    barrier = pltpu.get_barrier_semaphore()
    for to in (yp, ym, xp, xm, zp, zm, sib):
        pl.semaphore_signal(barrier, inc=1, device_id=to, device_id_type=MESH)
    own_x = pltpu.make_async_copy(tok, xg.at[0, zh, c, y], load_sem.at[0])
    own_g = pltpu.make_async_copy(cot, xg.at[1, zh, c, y], load_sem.at[1])
    w_gate = pltpu.make_async_copy(gate, wgu.at[pl.ds(0, 384)], load_sem.at[2])
    w_up = pltpu.make_async_copy(up, wgu.at[pl.ds(384, 384)], load_sem.at[3])
    w_down = pltpu.make_async_copy(down, wd, load_sem.at[4])


    def send(ref, to, kind, name_there, source=None):
        pltpu.make_async_remote_copy(
            ref if source is None else source, ref, sent_sem.at[kind], recv_sem[name_there],
            device_id=to, device_id_type=MESH).start()

    def landed(ref, name):
        pltpu.make_async_remote_copy(
            ref, ref, sent_sem.at[0], recv_sem[name], device_id=sib, device_id_type=MESH).wait_recv()

    def sent(ref, kind):
        pltpu.make_async_remote_copy(
            ref, ref, sent_sem.at[kind], recv_sem[("lz",)], device_id=sib, device_id_type=MESH).wait_send()

    def eighth(rel, s):
        q = 2 * (s // 2 % 2) + (par if rel == 0 else 1 - par)
        return pl.ds(pl.multiple_of(q * 1024 + s % 2 * 512, 512), 512)

    def piece(dz, dy, rel, s):
        zz = zh if dz == 0 else 1 - zh
        return xg.at[s // 4, zz, c, (y + dy) % 4, :, eighth(rel, s)]

    def group(dz, rel, s, cc):
        zz = zh if dz == 0 else 1 - zh
        q = 2 * (s % 2) + (par if rel == 0 else 1 - par)
        return xg.at[s // 2, zz, cc, :, :, pl.ds(pl.multiple_of(q * 1024, 1024), 1024)]

    DY = {"m": 3, "p": 1, "2": 2}

    def given(rel, s):
        return (tok, cot)[s // 4].at[:, eighth(rel, s)]

    def spread_y(dz, s):
        source = given(0, s) if dz == 0 else None
        send(piece(dz, 0, 0, s), yp, 0, ("y", dz, "m", s), source)
        send(piece(dz, 0, 0, s), ym, 0, ("y", dz, "p", s), source)

    def share_x(dz, who, s):
        forward = {"m": True, "p": False, "2": s % 2 == 0}[who]
        forward = forward if s < 4 else not forward
        send(piece(dz, DY[who], 0, s), xp if forward else xm, 0, ("x", dz, s // 2))

    def on_y(dz, who, s):
        landed(piece(dz, DY[who], 0, s), ("y", dz, who, s))
        if who == "m" and s % 2 == 0:
            send(piece(dz, DY[who], 0, s), yp, 0, ("y", dz, "2", s))
        if who == "p" and s % 2 == 1:
            send(piece(dz, DY[who], 0, s), ym, 0, ("y", dz, "2", s))
        share_x(dz, who, s)

    def at_edge(like, to, kind, name_there, source=None, arrived=None):
        @pl.when(edge)
        def _():
            if arrived is not None:
                landed(like(), arrived)
            send(like(), to, kind, name_there, source)

    def quarter_of(rel, quarter):
        q = 2 * (quarter % 2) + (par if rel == 0 else 1 - par)
        return pl.ds(pl.multiple_of(q * 1024, 1024), 1024)

    def other_own(quarter):
        return xg.at[quarter // 2, 1 - zh, c, y, :, quarter_of(1, quarter)]

    def z_edge(rel, quarter):
        if rel == 1:
            at_edge(lambda: other_own(quarter), inn, 2, ("z1", quarter), arrived=("z1", quarter))
            return
        for s in (2 * quarter, 2 * quarter + 1):
            at_edge(lambda s=s: piece(1, 0, 0, s), inn, 2, ("z", s), arrived=("z", s))

    def z_in(s):
        pl.when(~edge)(lambda: landed(piece(1, 0, 0, s), ("z", s)))

    def z_inner(quarter):
        pl.when(~edge)(lambda: landed(other_own(quarter), ("z1", quarter)))

    def to_sibling(dz, rel, s):
        k = dz * 8 + rel * 4 + s
        cp = pltpu.make_async_remote_copy(
            group(dz, rel, s, c), group(dz, rel, s, c), sent_sem.at[1], in_sem.at[k], device_id=sib, device_id_type=MESH)
        cp.start()

    def multiply(step):
        dz, rel, s = step // 8, step // 4 % 2, step % 4
        zz = jnp.where(dz == 0, zh, 1 - zh)
        q = 2 * (s % 2) + jnp.where(rel == 0, par, 1 - par)
        cols = pl.ds(pl.multiple_of(q * 1024, 1024), 1024)
        arrived = xg.at[s // 2, zz, 1 - c, :, :, cols]
        pltpu.make_async_remote_copy(
            arrived, arrived, sent_sem.at[1], in_sem.at[step], device_id=sib, device_id_type=MESH).wait_recv()

        def add(arr, w, acc):
            rows = xg[arr, zz, :, :, :, cols].reshape(256, 1024)
            size = 256 if arr == 0 else 384
            for m in range(0, w.shape[0], size):
                at = pl.ds(m, size)
                acc[dz, at, :] += lax.dot_general(w[at, cols], rows, NT, preferred_element_type=jnp.float32)

        pl.when(s < 2)(lambda: add(0, wgu, accx))
        pl.when(s >= 2)(lambda: add(1, wd, accg))

    def lblock(dz, dy):
        return lmat.at[zh if dz == 0 else 1 - zh, c, (y + dy) % 4]

    def l_spread(dz):
        send(lblock(dz, 0), yp, 3, ("ly", dz, "m"))
        send(lblock(dz, 0), ym, 3, ("ly", dz, "p"))

    def l_on_y(dz):
        landed(lblock(dz, 3), ("ly", dz, "m"))
        send(lblock(dz, 3), yp, 3, ("ly", dz, "2"))
        landed(lblock(dz, 1), ("ly", dz, "p"))

    def lgroup(dz, cc):
        return lmat.at[zh if dz == 0 else 1 - zh, cc]

    def l_sibling(dz):
        landed(lblock(dz, 2), ("ly", dz, "2"))
        send(lgroup(dz, c), sib, 4, ("lc", dz))

    def l_done(dz):
        landed(lgroup(dz, 1 - c), ("lc", dz))

    def greet(k):
        pl.semaphore_signal(met.at[2 * k], inc=1, device_id=zp, device_id_type=MESH)
        pl.semaphore_signal(met.at[2 * k + 1], inc=1, device_id=zm, device_id_type=MESH)

    def greeted(k):
        pl.semaphore_wait(met.at[2 * k], 1)
        pl.semaphore_wait(met.at[2 * k + 1], 1)

    def halves(quarter):
        return (2 * quarter, 2 * quarter + 1)

    def on_y_both(dz, quarter):
        for s in halves(quarter):
            on_y(dz, "m", s)
            on_y(dz, "p", s)

    def on_y2(dz, quarter):
        for s in halves(quarter):
            landed(piece(dz, 2, 0, s), ("y", dz, "2", s))
            share_x(dz, "2", s)
        to_sibling(dz, 0, quarter)

    def on_x_all(dz, quarter):
        landed(xg.at[0, 0, 0, pl.ds(0, 3), :, pl.ds(0, 1024)], ("x", dz, quarter))
        to_sibling(dz, 1, quarter)

    def l_edge():
        at_edge(lambda: lblock(1, 0), inn, 5, ("lz",), arrived=("lz",))

    def l_on_z():
        pl.when(~edge)(lambda: landed(lblock(1, 0), ("lz",)))
        l_spread(1)

    def own(quarter):
        for s in halves(quarter):
            spread_y(0, s)
            at_edge(lambda s=s: piece(0, 0, 0, s), outn, 2, ("z", s), given(0, s))

    def own_rest(quarter):
        cols = quarter_of(1, quarter)
        at_edge(lambda: xg.at[quarter // 2, zh, c, y, :, cols], outn, 2, ("z1", quarter), (tok, cot)[quarter // 2].at[:, cols])

    def other(quarter):
        for s in halves(quarter):
            z_in(s)
            spread_y(1, s)

    half = lax.broadcasted_iota(jnp.int32, (8, 256), 0) < 4

    def over_experts(v, op):
        t = op(v, axis=0)
        a = op(t[0:4], axis=0, keepdims=True)
        b = op(t[4:8], axis=0, keepdims=True)
        return jnp.where(half, a, b)

    def softmax():
        l_done(0)
        l_done(1)
        for zz in range(2):
            flipped = lmat[zz].reshape(256, 128).T
            for k in range(16):
                probs[k, pl.ds(zz * 4, 4), :] = flipped[k * 4 : k * 4 + 4]
                chosen[k, pl.ds(zz * 4, 4), :] = flipped[64 + k * 4 : 68 + k * 4]
        raw = probs[...]
        raised = jnp.exp(raw - over_experts(raw, jnp.max))
        probs[...] = raised / over_experts(raised, jnp.sum)

    expert = lax.broadcasted_iota(jnp.int32, (64, 32), 0)
    picked = jnp.zeros((64, 32), jnp.float32)
    for k in range(8):
        picked += (routes[k : k + 1, :] == expert).astype(jnp.float32)
    lmat[zh, c, y, :, pl.ds(0, 64)] = logits[...]
    lmat[zh, c, y, :, pl.ds(64, 64)] = picked.T
    pl.semaphore_wait(barrier, 7)
    own(0)
    l_spread(0)
    at_edge(lambda: lblock(0, 0), outn, 5, ("lz",))
    for s in range(1, 4):
        own(s)
    for s in range(4):
        own_rest(s)
    for cp in (own_x, own_g, w_gate, w_up, w_down):
        cp.start()
    greet(0)
    accx[...] = jnp.zeros_like(accx)
    accg[...] = jnp.zeros_like(accg)
    own_x.wait()
    own_g.wait()
    on_y_both(0, 0)
    l_edge()
    z_edge(0, 0)
    on_y_both(0, 1)
    z_edge(0, 1)
    l_on_y(0)
    greeted(0)
    greet(1)
    on_y_both(0, 2)
    z_edge(0, 2)
    other(0)
    l_on_z()
    on_y_both(0, 3)
    z_edge(0, 3)
    other(1)
    on_y2(0, 0)
    greeted(1)
    greet(2)
    on_y2(0, 1)
    other(2)
    z_edge(1, 0)
    on_y_both(1, 0)
    on_y2(0, 2)
    other(3)
    z_edge(1, 1)
    w_gate.wait()
    w_up.wait()
    w_down.wait()

    def before_1():
        on_y_both(1, 1)
        on_y2(0, 3)
        z_edge(1, 2)
        l_sibling(0)
        on_x_all(0, 0)

    def before_2():
        z_edge(1, 3)
        on_x_all(0, 1)

    def before_3():
        on_y_both(1, 2)
        on_x_all(0, 2)
        l_on_y(1)

    def before_5():
        on_y_both(1, 3)
        on_y2(1, 0)
        on_x_all(0, 3)

    def before_6():
        on_y2(1, 1)
        greeted(2)
        l_sibling(1)

    def before_8():
        on_y2(1, 2)

    def before_10():
        on_y2(1, 3)
        z_inner(0)
        on_x_all(1, 0)
        softmax()

    def before_11():
        z_inner(1)
        on_x_all(1, 1)

    def before_12():
        z_inner(2)
        on_x_all(1, 2)

    def before_13():
        z_inner(3)
        on_x_all(1, 3)

    before = {1: before_1, 2: before_2, 3: before_3, 5: before_5, 6: before_6, 8: before_8,
              10: before_10, 11: before_11, 12: before_12, 13: before_13}

    def at_step(step, low, high):
        if not any(low <= k < high for k in before):
            return
        if high - low == 1:
            before[low]()
            return
        mid = (low + high) // 2
        lax.cond(step < mid, lambda: at_step(step, low, mid), lambda: at_step(step, mid, high))

    @pl.loop(0, 16)
    def _(step):
        at_step(step, 0, 16)
        multiply(jnp.where(step == 11, 12, jnp.where(step == 12, 11, step)))

    def local_scores(dz):
        g = accx[dz, 0:384, :]
        hidden = g / (1.0 + jnp.exp(-g)) * accx[dz, 384:768, :]
        both = hidden * accg[dz]
        return jnp.concatenate([jnp.sum(both[k * 96 : k * 96 + 96], axis=0, keepdims=True) for k in range(4)], axis=0)

    here, there = local_scores(0), local_scores(1)
    part[...] = jnp.where(zh == 0, jnp.concatenate([here, there], 0), jnp.concatenate([there, here], 0))

    def exchange(kind, source, place, peers):
        for k, to in peers:
            pltpu.make_async_remote_copy(
                source, place(k), sent_sem.at[kind], recv_sem[("t", kind)], device_id=to, device_id_type=MESH).start()

    exchange(6, part, lambda k: got_y.at[k], [
        (dy * 2 + dc, dev(x, (y + dy) % 4, z, (c + dc) % 2)) for dy, dc in ((2, 1), (2, 0), (1, 1), (3, 1), (1, 0), (3, 0), (0, 1))])
    landed(got_y.at[pl.ds(1, 7)], ("t", 6))
    total[...] = part[...] + sum(got_y[k] for k in range(1, 8))
    exchange(7, total, lambda k: got_z.at[k], [(k, dev(x, y, (z + k) % 8, c)) for k in (4, 3, 5, 2, 6, 1, 7)])
    landed(got_z.at[pl.ds(1, 7)], ("t", 7))
    for k in range(4):
        first = total[...] if k == 0 else got_z[k]
        got2[x * 4 + (z + 8 - k) % 4] = first + got_z[k + 4]
    mine = got2.at[pl.ds(x * 4, 4)]
    exchange(8, mine, lambda k: mine, [(k, dev((x + k) % 4, y, z, c)) for k in (2, 1, 3)])
    landed(got2.at[pl.ds(0, 12)], ("t", 8))

    scores = got2[...]
    pr, ch = probs[...], chosen[...]
    kept = pr * ch
    mass = over_experts(kept, jnp.sum)
    weighted = over_experts(kept * scores, jnp.sum)
    prob_grad = scores / mass - ch * (weighted / (mass * mass))
    grad = pr * (prob_grad - over_experts(pr * prob_grad, jnp.sum))
    for k in range(16):
        lgc[0, pl.ds(k * 4, 4), :] = grad[k, 0:4]
        lgc[1, pl.ds(k * 4, 4), :] = grad[k, 4:8]
    turned[...] = lgc[zh].T
    lg_out[...] = turned[pl.ds(c * 128 + y * 32, 32), :]
    cols = pl.ds(pl.multiple_of(d * 256, 256), 256)
    rg = jnp.zeros((64, 256), jnp.float32)
    for zz in range(2):
        rows = xg[0, zz, :, :, :, cols].reshape(256, 256)
        rg += jnp.dot(lgc[zz].astype(jnp.bfloat16), rows, preferred_element_type=jnp.float32)
    rg_out[...] = rg

    sent(wd, 0)
    sent(xg.at[0], 1)
    sent(got2.at[pl.ds(0, 12)], 3)
    sent(got2, 4)
    sent(got_y.at[pl.ds(1, 7)], 6)
    sent(got_z.at[pl.ds(1, 7)], 7)
    sent(got2.at[pl.ds(0, 12)], 8)

    @pl.when(edge)
    def _():
        sent(xg.at[0, 0, 0], 2)
        sent(got2.at[pl.ds(0, 4)], 5)


N_RECV = 80


def finish(lg, rg, lg_out, rg_out):
    lg_out[...] = lg[...]
    rg_out[...] = rg[...]


def per_device(tokens, cotangent, logits, routes, gate_weight, up_weight, down_weight):
    flat = [w.reshape(384, 4096) for w in (gate_weight, up_weight, down_weight)]
    hbm, vmem = pl.BlockSpec(memory_space=pl.ANY), pl.BlockSpec(memory_space=pltpu.VMEM)
    f32, bf16 = jnp.float32, jnp.bfloat16
    logit_grad, router_grad = pl.pallas_call(
        kernel,
        out_shape=(jax.ShapeDtypeStruct((32, 64), f32), jax.ShapeDtypeStruct((64, 256), f32)),
        in_specs=[hbm, hbm, vmem, vmem, hbm, hbm, hbm],
        out_specs=(vmem, vmem),
        scratch_shapes=[
            pltpu.VMEM((2, 2, 2, 4, 32, 4096), bf16),
            pltpu.VMEM((768, 4096), bf16),
            pltpu.VMEM((384, 4096), bf16),
            pltpu.VMEM((2, 768, 256), f32),
            pltpu.VMEM((2, 384, 256), f32),
            pltpu.VMEM((2, 2, 4, 32, 128), f32),
            pltpu.VMEM((16, 8, 256), f32),
            pltpu.VMEM((16, 8, 256), f32),
            pltpu.VMEM((8, 256), f32),
            pltpu.VMEM((8, 256), f32),
            pltpu.VMEM((8, 8, 256), f32),
            pltpu.VMEM((8, 8, 256), f32),
            pltpu.VMEM((16, 8, 256), f32),
            pltpu.VMEM((2, 64, 256), f32),
            pltpu.VMEM((256, 64), f32),
            pltpu.SemaphoreType.DMA((5,)),
            pltpu.SemaphoreType.DMA((9,)),
            pltpu.SemaphoreType.DMA((N_RECV,)),
            pltpu.SemaphoreType.DMA((16,)),
            pltpu.SemaphoreType.REGULAR((6,)),
        ],
        compiler_params=pltpu.CompilerParams(
            collective_id=0, has_side_effects=True, vmem_limit_bytes=60 * MIB),
        cost_estimate=pl.CostEstimate(flops=2 * 512 * 384 * 4096 * 3, bytes_accessed=10 * MIB, transcendentals=512 * 384),
        name="router_grad",
    )(tokens, cotangent, logits, routes.T, *flat)
    logit_grad, router_grad = pl.pallas_call(
        finish,
        out_shape=(jax.ShapeDtypeStruct((32, 64), f32), jax.ShapeDtypeStruct((64, 256), f32)),
        in_specs=[vmem, vmem],
        out_specs=(vmem, vmem),
        name="finish",
    )(logit_grad, router_grad)
    return logit_grad, router_grad.T


def solution(mesh):
    rows = P("dp", None)
    placed = (rows, rows, rows, rows) + (P("expert", "dp", None),) * 3
    return jax.shard_map(
        per_device, mesh=mesh, in_specs=placed, out_specs=(rows, rows), check_vma=False)
```

```python
import jax
import jax.numpy as jnp
from jax import lax
from jax.experimental import pallas as pl
from jax.experimental.pallas import tpu as pltpu
from jax.sharding import PartitionSpec as P

MESH = pl.DeviceIdType.MESH
MIB = 1024 * 1024
NT = (((1,), (1,)), ((), ()))


class Sems:
    def __init__(self, ref):
        self.ref, self.names = ref, {}

    def __getitem__(self, name):
        k = self.names.setdefault(name, len(self.names))
        assert k < N_RECV
        return self.ref.at[k]


def kernel(tok, cot, logits, routes, gate, up, down, lg_out, rg_out,
           xg, wgu, wd, accx, accg, lmat, probs, chosen, part, total, got_y, got_z, got2, lgc, turned,
           load_sem, sent_sem, recv_ref, in_sem, met):
    d = lax.axis_index("dp")
    e = lax.axis_index("expert")
    y, zh, c = d // 4, (d // 2) % 2, d % 2
    x, zl = e // 4, e % 4
    z = zh * 4 + zl
    par = x % 2
    recv_sem = Sems(recv_ref)

    def dev(x_, y_, z_, c_):
        return ((y_ * 2 + z_ // 4) * 2 + c_, x_ * 4 + z_ % 4)

    xp, xm = dev((x + 1) % 4, y, z, c), dev((x + 3) % 4, y, z, c)
    yp, ym = dev(x, (y + 1) % 4, z, c), dev(x, (y + 3) % 4, z, c)
    zp, zm = dev(x, y, (z + 1) % 8, c), dev(x, y, (z + 7) % 8, c)
    low = zl < 2
    outn = tuple(jnp.where(low, a, b) for a, b in zip(zm, zp))
    inn = tuple(jnp.where(low, a, b) for a, b in zip(zp, zm))
    sib = dev(x, y, z, 1 - c)
    edge = (zl == 0) | (zl == 3)

    barrier = pltpu.get_barrier_semaphore()
    for to in (yp, ym, xp, xm, zp, zm, sib):
        pl.semaphore_signal(barrier, inc=1, device_id=to, device_id_type=MESH)
    own_x = pltpu.make_async_copy(tok, xg.at[0, zh, c, y], load_sem.at[0])
    own_g = pltpu.make_async_copy(cot, xg.at[1, zh, c, y], load_sem.at[1])
    w_gate = pltpu.make_async_copy(gate, wgu.at[pl.ds(0, 384)], load_sem.at[2])
    w_up = pltpu.make_async_copy(up, wgu.at[pl.ds(384, 384)], load_sem.at[3])
    w_down = pltpu.make_async_copy(down, wd, load_sem.at[4])


    def send(ref, to, kind, name_there, source=None):
        pltpu.make_async_remote_copy(
            ref if source is None else source, ref, sent_sem.at[kind], recv_sem[name_there],
            device_id=to, device_id_type=MESH).start()

    def landed(ref, name):
        pltpu.make_async_remote_copy(
            ref, ref, sent_sem.at[0], recv_sem[name], device_id=sib, device_id_type=MESH).wait_recv()

    def sent(ref, kind):
        pltpu.make_async_remote_copy(
            ref, ref, sent_sem.at[kind], recv_sem[("lz",)], device_id=sib, device_id_type=MESH).wait_send()

    def eighth(rel, s):
        q = 2 * (s // 2 % 2) + (par if rel == 0 else 1 - par)
        return pl.ds(pl.multiple_of(q * 1024 + s % 2 * 512, 512), 512)

    def piece(dz, dy, rel, s):
        zz = zh if dz == 0 else 1 - zh
        return xg.at[s // 4, zz, c, (y + dy) % 4, :, eighth(rel, s)]

    def group(dz, rel, s, cc):
        zz = zh if dz == 0 else 1 - zh
        q = 2 * (s % 2) + (par if rel == 0 else 1 - par)
        return xg.at[s // 2, zz, cc, :, :, pl.ds(pl.multiple_of(q * 1024, 1024), 1024)]

    DY = {"m": 3, "p": 1, "2": 2}

    def given(rel, s):
        return (tok, cot)[s // 4].at[:, eighth(rel, s)]

    def spread_y(dz, s):
        source = given(0, s) if dz == 0 else None
        send(piece(dz, 0, 0, s), yp, 0, ("y", dz, "m", s), source)
        send(piece(dz, 0, 0, s), ym, 0, ("y", dz, "p", s), source)

    def share_x(dz, who, s):
        forward = {"m": True, "p": False, "2": s % 2 == 0}[who]
        forward = forward if s < 4 else not forward
        send(piece(dz, DY[who], 0, s), xp if forward else xm, 0, ("x", dz, s // 2))

    def on_y(dz, who, s):
        landed(piece(dz, DY[who], 0, s), ("y", dz, who, s))
        if who == "m" and s % 2 == 0:
            send(piece(dz, DY[who], 0, s), yp, 0, ("y", dz, "2", s))
        if who == "p" and s % 2 == 1:
            send(piece(dz, DY[who], 0, s), ym, 0, ("y", dz, "2", s))
        share_x(dz, who, s)

    def at_edge(like, to, kind, name_there, source=None, arrived=None):
        @pl.when(edge)
        def _():
            if arrived is not None:
                landed(like(), arrived)
            send(like(), to, kind, name_there, source)

    def quarter_of(rel, quarter):
        q = 2 * (quarter % 2) + (par if rel == 0 else 1 - par)
        return pl.ds(pl.multiple_of(q * 1024, 1024), 1024)

    def other_own(quarter):
        return xg.at[quarter // 2, 1 - zh, c, y, :, quarter_of(1, quarter)]

    def z_edge(rel, quarter):
        if rel == 1:
            at_edge(lambda: other_own(quarter), inn, 2, ("z1", quarter), arrived=("z1", quarter))
            return
        for s in (2 * quarter, 2 * quarter + 1):
            at_edge(lambda s=s: piece(1, 0, 0, s), inn, 2, ("z", s), arrived=("z", s))

    def z_in(s):
        pl.when(~edge)(lambda: landed(piece(1, 0, 0, s), ("z", s)))

    def z_inner(quarter):
        pl.when(~edge)(lambda: landed(other_own(quarter), ("z1", quarter)))

    def to_sibling(dz, rel, s):
        k = dz * 8 + rel * 4 + s
        cp = pltpu.make_async_remote_copy(
            group(dz, rel, s, c), group(dz, rel, s, c), sent_sem.at[1], in_sem.at[k], device_id=sib, device_id_type=MESH)
        cp.start()

    def multiply(step):
        dz, rel, s = step // 8, step // 4 % 2, step % 4
        zz = jnp.where(dz == 0, zh, 1 - zh)
        q = 2 * (s % 2) + jnp.where(rel == 0, par, 1 - par)
        cols = pl.ds(pl.multiple_of(q * 1024, 1024), 1024)
        arrived = xg.at[s // 2, zz, 1 - c, :, :, cols]
        pltpu.make_async_remote_copy(
            arrived, arrived, sent_sem.at[1], in_sem.at[step], device_id=sib, device_id_type=MESH).wait_recv()

        def add(arr, w, acc):
            rows = xg[arr, zz, :, :, :, cols].reshape(256, 1024)
            size = 256 if arr == 0 else 384
            for m in range(0, w.shape[0], size):
                at = pl.ds(m, size)
                acc[dz, at, :] += lax.dot_general(w[at, cols], rows, NT, preferred_element_type=jnp.float32)

        pl.when(s < 2)(lambda: add(0, wgu, accx))
        pl.when(s >= 2)(lambda: add(1, wd, accg))

    def lblock(dz, dy):
        return lmat.at[zh if dz == 0 else 1 - zh, c, (y + dy) % 4]

    def l_spread(dz):
        send(lblock(dz, 0), yp, 3, ("ly", dz, "m"))
        send(lblock(dz, 0), ym, 3, ("ly", dz, "p"))

    def l_on_y(dz):
        landed(lblock(dz, 3), ("ly", dz, "m"))
        send(lblock(dz, 3), yp, 3, ("ly", dz, "2"))
        landed(lblock(dz, 1), ("ly", dz, "p"))

    def lgroup(dz, cc):
        return lmat.at[zh if dz == 0 else 1 - zh, cc]

    def l_sibling(dz):
        landed(lblock(dz, 2), ("ly", dz, "2"))
        send(lgroup(dz, c), sib, 4, ("lc", dz))

    def l_done(dz):
        landed(lgroup(dz, 1 - c), ("lc", dz))

    def greet(k):
        pl.semaphore_signal(met.at[2 * k], inc=1, device_id=zp, device_id_type=MESH)
        pl.semaphore_signal(met.at[2 * k + 1], inc=1, device_id=zm, device_id_type=MESH)

    def greeted(k):
        pl.semaphore_wait(met.at[2 * k], 1)
        pl.semaphore_wait(met.at[2 * k + 1], 1)

    def halves(quarter):
        return (2 * quarter, 2 * quarter + 1)

    def on_y_both(dz, quarter):
        for s in halves(quarter):
            on_y(dz, "m", s)
            on_y(dz, "p", s)

    def on_y2(dz, quarter):
        for s in halves(quarter):
            landed(piece(dz, 2, 0, s), ("y", dz, "2", s))
            share_x(dz, "2", s)
        to_sibling(dz, 0, quarter)

    def on_x_all(dz, quarter):
        landed(xg.at[0, 0, 0, pl.ds(0, 3), :, pl.ds(0, 1024)], ("x", dz, quarter))
        to_sibling(dz, 1, quarter)

    def l_edge():
        at_edge(lambda: lblock(1, 0), inn, 5, ("lz",), arrived=("lz",))

    def l_on_z():
        pl.when(~edge)(lambda: landed(lblock(1, 0), ("lz",)))
        l_spread(1)

    def own(quarter):
        for s in halves(quarter):
            spread_y(0, s)
            at_edge(lambda s=s: piece(0, 0, 0, s), outn, 2, ("z", s), given(0, s))

    def own_rest(quarter):
        cols = quarter_of(1, quarter)
        at_edge(lambda: xg.at[quarter // 2, zh, c, y, :, cols], outn, 2, ("z1", quarter), (tok, cot)[quarter // 2].at[:, cols])

    def other(quarter):
        for s in halves(quarter):
            z_in(s)
            spread_y(1, s)

    half = lax.broadcasted_iota(jnp.int32, (8, 256), 0) < 4

    def over_experts(v, op):
        t = op(v, axis=0)
        a = op(t[0:4], axis=0, keepdims=True)
        b = op(t[4:8], axis=0, keepdims=True)
        return jnp.where(half, a, b)

    def softmax():
        l_done(0)
        l_done(1)
        for zz in range(2):
            flipped = lmat[zz].reshape(256, 128).T
            for k in range(16):
                probs[k, pl.ds(zz * 4, 4), :] = flipped[k * 4 : k * 4 + 4]
                chosen[k, pl.ds(zz * 4, 4), :] = flipped[64 + k * 4 : 68 + k * 4]
        raw = probs[...]
        raised = jnp.exp(raw - over_experts(raw, jnp.max))
        probs[...] = raised / over_experts(raised, jnp.sum)

    pl.semaphore_wait(barrier, 7)
    own(0)
    own(1)
    for cp in (own_x, own_g, w_gate, w_up, w_down):
        cp.start()
    expert = lax.broadcasted_iota(jnp.int32, (64, 32), 0)
    picked = jnp.zeros((64, 32), jnp.float32)
    for k in range(8):
        picked += (routes[k : k + 1, :] == expert).astype(jnp.float32)
    lmat[zh, c, y, :, pl.ds(0, 64)] = logits[...]
    lmat[zh, c, y, :, pl.ds(64, 64)] = picked.T
    l_spread(0)
    at_edge(lambda: lblock(0, 0), outn, 5, ("lz",))
    own(2)
    own(3)
    for s in range(4):
        own_rest(s)
    greet(0)
    accx[...] = jnp.zeros_like(accx)
    accg[...] = jnp.zeros_like(accg)
    own_x.wait()
    own_g.wait()
    on_y_both(0, 0)
    z_edge(0, 0)
    on_y_both(0, 1)
    z_edge(0, 1)
    l_edge()
    greeted(0)
    greet(1)
    on_y_both(0, 2)
    z_edge(0, 2)
    l_on_y(0)
    other(0)
    on_y_both(0, 3)
    z_edge(0, 3)
    other(1)
    l_on_z()
    on_y2(0, 0)
    greeted(1)
    greet(2)
    on_y2(0, 1)
    other(2)
    z_edge(1, 0)
    on_y_both(1, 0)
    on_y2(0, 2)
    other(3)
    z_edge(1, 1)
    w_gate.wait()
    w_up.wait()
    w_down.wait()

    def before_1():
        on_y_both(1, 1)
        on_y2(0, 3)
        z_edge(1, 2)
        l_sibling(0)
        on_x_all(0, 0)

    def before_2():
        z_edge(1, 3)
        on_x_all(0, 1)

    def before_3():
        on_y_both(1, 2)
        on_x_all(0, 2)
        l_on_y(1)

    def before_5():
        on_y_both(1, 3)
        on_y2(1, 0)
        on_x_all(0, 3)

    def before_6():
        on_y2(1, 1)
        greeted(2)
        l_sibling(1)

    def before_8():
        on_y2(1, 2)

    def before_10():
        on_y2(1, 3)
        z_inner(0)
        on_x_all(1, 0)
        softmax()

    def before_11():
        z_inner(1)
        on_x_all(1, 1)

    def before_12():
        z_inner(2)
        on_x_all(1, 2)

    def before_13():
        z_inner(3)
        on_x_all(1, 3)

    before = {1: before_1, 2: before_2, 3: before_3, 5: before_5, 6: before_6, 8: before_8,
              10: before_10, 11: before_11, 12: before_12, 13: before_13}

    def at_step(step, low, high):
        if not any(low <= k < high for k in before):
            return
        if high - low == 1:
            before[low]()
            return
        mid = (low + high) // 2
        lax.cond(step < mid, lambda: at_step(step, low, mid), lambda: at_step(step, mid, high))

    @pl.loop(0, 16)
    def _(step):
        at_step(step, 0, 16)
        multiply(jnp.where(step == 11, 12, jnp.where(step == 12, 11, step)))

    def local_scores(dz):
        g = accx[dz, 0:384, :]
        hidden = g / (1.0 + jnp.exp(-g)) * accx[dz, 384:768, :]
        both = hidden * accg[dz]
        return jnp.concatenate([jnp.sum(both[k * 96 : k * 96 + 96], axis=0, keepdims=True) for k in range(4)], axis=0)

    here, there = local_scores(0), local_scores(1)
    part[...] = jnp.where(zh == 0, jnp.concatenate([here, there], 0), jnp.concatenate([there, here], 0))

    def exchange(kind, source, place, peers):
        for k, to in peers:
            pltpu.make_async_remote_copy(
                source, place(k), sent_sem.at[kind], recv_sem[("t", kind)], device_id=to, device_id_type=MESH).start()

    exchange(6, part, lambda k: got_y.at[k], [
        (dy * 2 + dc, dev(x, (y + dy) % 4, z, (c + dc) % 2)) for dy, dc in ((2, 1), (2, 0), (1, 1), (3, 1), (1, 0), (3, 0), (0, 1))])
    landed(got_y.at[pl.ds(1, 7)], ("t", 6))
    total[...] = part[...] + sum(got_y[k] for k in range(1, 8))
    exchange(7, total, lambda k: got_z.at[k], [(k, dev(x, y, (z + k) % 8, c)) for k in (4, 3, 5, 2, 6, 1, 7)])
    landed(got_z.at[pl.ds(1, 7)], ("t", 7))
    for k in range(4):
        first = total[...] if k == 0 else got_z[k]
        got2[x * 4 + (z + 8 - k) % 4] = first + got_z[k + 4]
    mine = got2.at[pl.ds(x * 4, 4)]
    exchange(8, mine, lambda k: mine, [(k, dev((x + k) % 4, y, z, c)) for k in (2, 1, 3)])
    landed(got2.at[pl.ds(0, 12)], ("t", 8))

    scores = got2[...]
    pr, ch = probs[...], chosen[...]
    kept = pr * ch
    mass = over_experts(kept, jnp.sum)
    weighted = over_experts(kept * scores, jnp.sum)
    prob_grad = scores / mass - ch * (weighted / (mass * mass))
    grad = pr * (prob_grad - over_experts(pr * prob_grad, jnp.sum))
    for k in range(16):
        lgc[0, pl.ds(k * 4, 4), :] = grad[k, 0:4]
        lgc[1, pl.ds(k * 4, 4), :] = grad[k, 4:8]
    turned[...] = lgc[zh].T
    lg_out[...] = turned[pl.ds(c * 128 + y * 32, 32), :]
    cols = pl.ds(pl.multiple_of(d * 256, 256), 256)
    rg = jnp.zeros((64, 256), jnp.float32)
    for zz in range(2):
        rows = xg[0, zz, :, :, :, cols].reshape(256, 256)
        rg += jnp.dot(lgc[zz].astype(jnp.bfloat16), rows, preferred_element_type=jnp.float32)
    rg_out[...] = rg

    sent(wd, 0)
    sent(xg.at[0], 1)
    sent(got2.at[pl.ds(0, 12)], 3)
    sent(got2, 4)
    sent(got_y.at[pl.ds(1, 7)], 6)
    sent(got_z.at[pl.ds(1, 7)], 7)
    sent(got2.at[pl.ds(0, 12)], 8)

    @pl.when(edge)
    def _():
        sent(xg.at[0, 0, 0], 2)
        sent(got2.at[pl.ds(0, 4)], 5)


N_RECV = 80


def finish(lg, rg, lg_out, rg_out):
    lg_out[...] = lg[...]
    rg_out[...] = rg[...]


def per_device(tokens, cotangent, logits, routes, gate_weight, up_weight, down_weight):
    flat = [w.reshape(384, 4096) for w in (gate_weight, up_weight, down_weight)]
    hbm, vmem = pl.BlockSpec(memory_space=pl.ANY), pl.BlockSpec(memory_space=pltpu.VMEM)
    f32, bf16 = jnp.float32, jnp.bfloat16
    logit_grad, router_grad = pl.pallas_call(
        kernel,
        out_shape=(pltpu.VMEM((32, 64), f32), pltpu.VMEM((64, 256), f32)),
        in_specs=[hbm, hbm, vmem, vmem, hbm, hbm, hbm],
        out_specs=(vmem, vmem),
        scratch_shapes=[
            pltpu.VMEM((2, 2, 2, 4, 32, 4096), bf16),
            pltpu.VMEM((768, 4096), bf16),
            pltpu.VMEM((384, 4096), bf16),
            pltpu.VMEM((2, 768, 256), f32),
            pltpu.VMEM((2, 384, 256), f32),
            pltpu.VMEM((2, 2, 4, 32, 128), f32),
            pltpu.VMEM((16, 8, 256), f32),
            pltpu.VMEM((16, 8, 256), f32),
            pltpu.VMEM((8, 256), f32),
            pltpu.VMEM((8, 256), f32),
            pltpu.VMEM((8, 8, 256), f32),
            pltpu.VMEM((8, 8, 256), f32),
            pltpu.VMEM((16, 8, 256), f32),
            pltpu.VMEM((2, 64, 256), f32),
            pltpu.VMEM((256, 64), f32),
            pltpu.SemaphoreType.DMA((5,)),
            pltpu.SemaphoreType.DMA((9,)),
            pltpu.SemaphoreType.DMA((N_RECV,)),
            pltpu.SemaphoreType.DMA((16,)),
            pltpu.SemaphoreType.REGULAR((6,)),
        ],
        compiler_params=pltpu.CompilerParams(
            collective_id=0, has_side_effects=True, vmem_limit_bytes=60 * MIB),
        cost_estimate=pl.CostEstimate(flops=2 * 512 * 384 * 4096 * 3, bytes_accessed=10 * MIB, transcendentals=512 * 384),
        name="router_grad",
    )(tokens, cotangent, logits, routes.T, *flat)
    logit_grad, router_grad = pl.pallas_call(
        finish,
        out_shape=(jax.ShapeDtypeStruct((32, 64), f32), jax.ShapeDtypeStruct((64, 256), f32)),
        in_specs=[vmem, vmem],
        out_specs=(vmem, vmem),
        name="finish",
    )(*(pltpu.with_memory_space_constraint(v, pltpu.VMEM) for v in (logit_grad, router_grad)))
    return logit_grad, router_grad.T


def solution(mesh):
    rows = P("dp", None)
    placed = (rows, rows, rows, rows) + (P("expert", "dp", None),) * 3
    return jax.shard_map(
        per_device, mesh=mesh, in_specs=placed, out_specs=(rows, rows), check_vma=False)
```

```python
import jax
import jax.numpy as jnp
from jax import lax
from jax.experimental import pallas as pl
from jax.experimental.pallas import tpu as pltpu
from jax.sharding import PartitionSpec as P

MESH = pl.DeviceIdType.MESH
MIB = 1024 * 1024
NT = (((1,), (1,)), ((), ()))


class Sems:
    def __init__(self, ref):
        self.ref, self.names = ref, {}

    def __getitem__(self, name):
        k = self.names.setdefault(name, len(self.names))
        assert k < N_RECV
        return self.ref.at[k]


def kernel(tok, cot, logits, routes, gate, up, down, lg_out, rg_out,
           xg, wgu, wd, accx, accg, lmat, probs, chosen, early, part, total, got_y, got_z, got2, lgc, turned,
           load_sem, sent_sem, recv_ref, in_sem, met):
    d = lax.axis_index("dp")
    e = lax.axis_index("expert")
    y, zh, c = d // 4, (d // 2) % 2, d % 2
    x, zl = e // 4, e % 4
    z = zh * 4 + zl
    par = x % 2
    recv_sem = Sems(recv_ref)

    def dev(x_, y_, z_, c_):
        return ((y_ * 2 + z_ // 4) * 2 + c_, x_ * 4 + z_ % 4)

    xp, xm = dev((x + 1) % 4, y, z, c), dev((x + 3) % 4, y, z, c)
    yp, ym = dev(x, (y + 1) % 4, z, c), dev(x, (y + 3) % 4, z, c)
    zp, zm = dev(x, y, (z + 1) % 8, c), dev(x, y, (z + 7) % 8, c)
    low = zl < 2
    outn = tuple(jnp.where(low, a, b) for a, b in zip(zm, zp))
    inn = tuple(jnp.where(low, a, b) for a, b in zip(zp, zm))
    sib = dev(x, y, z, 1 - c)
    edge = (zl == 0) | (zl == 3)

    barrier = pltpu.get_barrier_semaphore()
    for to in (yp, ym, xp, xm, zp, zm, sib):
        pl.semaphore_signal(barrier, inc=1, device_id=to, device_id_type=MESH)
    own_x = pltpu.make_async_copy(tok, xg.at[0, zh, c, y], load_sem.at[0])
    own_g = pltpu.make_async_copy(cot, xg.at[1, zh, c, y], load_sem.at[1])
    w_gate = pltpu.make_async_copy(gate, wgu.at[pl.ds(0, 384)], load_sem.at[2])
    w_up = pltpu.make_async_copy(up, wgu.at[pl.ds(384, 384)], load_sem.at[3])
    w_down = pltpu.make_async_copy(down, wd, load_sem.at[4])


    def send(ref, to, kind, name_there, source=None):
        pltpu.make_async_remote_copy(
            ref if source is None else source, ref, sent_sem.at[kind], recv_sem[name_there],
            device_id=to, device_id_type=MESH).start()

    def landed(ref, name):
        pltpu.make_async_remote_copy(
            ref, ref, sent_sem.at[0], recv_sem[name], device_id=sib, device_id_type=MESH).wait_recv()

    def sent(ref, kind):
        pltpu.make_async_remote_copy(
            ref, ref, sent_sem.at[kind], recv_sem[("lz",)], device_id=sib, device_id_type=MESH).wait_send()

    def eighth(rel, s):
        q = 2 * (s // 2 % 2) + (par if rel == 0 else 1 - par)
        return pl.ds(pl.multiple_of(q * 1024 + s % 2 * 512, 512), 512)

    def piece(dz, dy, rel, s):
        zz = zh if dz == 0 else 1 - zh
        return xg.at[s // 4, zz, c, (y + dy) % 4, :, eighth(rel, s)]

    def group(dz, rel, s, cc):
        zz = zh if dz == 0 else 1 - zh
        q = 2 * (s % 2) + (par if rel == 0 else 1 - par)
        return xg.at[s // 2, zz, cc, :, :, pl.ds(pl.multiple_of(q * 1024, 1024), 1024)]

    DY = {"m": 3, "p": 1, "2": 2}

    def given(rel, s):
        return (tok, cot)[s // 4].at[:, eighth(rel, s)]

    def spread_y(dz, s):
        source = given(0, s) if dz == 0 else None
        send(piece(dz, 0, 0, s), yp, 0, ("y", dz, s), source)
        send(piece(dz, 0, 0, s), ym, 0, ("y", dz, s), source)

    def share_x(dz, who, s):
        forward = {"m": True, "p": False, "2": s % 2 == 0}[who]
        forward = forward if s < 4 else not forward
        send(piece(dz, DY[who], 0, s), xp if forward else xm, 0, ("x", dz, s // 2 if (dz, s) != (1, 7) else 4))

    def on_y(dz, s):
        landed(xg.at[0, 0, 0, 0, :, pl.ds(0, 1024)], ("y", dz, s))
        who, to = ("m", yp) if s % 2 == 0 else ("p", ym)
        send(piece(dz, DY[who], 0, s), to, 0, ("y2", dz, s // 2))
        share_x(dz, "m", s)
        share_x(dz, "p", s)

    def at_edge(like, to, kind, name_there, source=None, arrived=None):
        @pl.when(edge)
        def _():
            if arrived is not None:
                landed(like(), arrived)
            send(like(), to, kind, name_there, source)

    def quarter_of(rel, quarter):
        q = 2 * (quarter % 2) + (par if rel == 0 else 1 - par)
        return pl.ds(pl.multiple_of(q * 1024, 1024), 1024)

    def other_own(quarter):
        return xg.at[quarter // 2, 1 - zh, c, y, :, quarter_of(1, quarter)]

    def z_edge(rel, quarter):
        if rel == 1:
            at_edge(lambda: other_own(quarter), inn, 2, ("z1", quarter), arrived=("z1", quarter))
            return
        for s in (2 * quarter, 2 * quarter + 1):
            at_edge(lambda s=s: piece(1, 0, 0, s), inn, 2, ("z", s), arrived=("z", s))

    def z_in(s):
        pl.when(~edge)(lambda: landed(piece(1, 0, 0, s), ("z", s)))

    def z_inner(quarter):
        pl.when(~edge)(lambda: landed(other_own(quarter), ("z1", quarter)))

    def to_sibling(dz, rel, s):
        k = dz * 8 + rel * 4 + s
        cp = pltpu.make_async_remote_copy(
            group(dz, rel, s, c), group(dz, rel, s, c), sent_sem.at[1], in_sem.at[k], device_id=sib, device_id_type=MESH)
        cp.start()

    def multiply(step):
        dz, rel, s = step // 8, step // 4 % 2, step % 4
        zz = jnp.where(dz == 0, zh, 1 - zh)
        q = 2 * (s % 2) + jnp.where(rel == 0, par, 1 - par)
        cols = pl.ds(pl.multiple_of(q * 1024, 1024), 1024)
        arrived = xg.at[s // 2, zz, 1 - c, :, :, cols]
        pltpu.make_async_remote_copy(
            arrived, arrived, sent_sem.at[1], in_sem.at[step], device_id=sib, device_id_type=MESH).wait_recv()

        def add(arr, w, acc):
            rows = xg[arr, zz, :, :, :, cols].reshape(256, 1024)
            size = 256 if arr == 0 else 384
            for m in range(0, w.shape[0], size):
                at = pl.ds(m, size)
                acc[dz, at, :] += lax.dot_general(w[at, cols], rows, NT, preferred_element_type=jnp.float32)

        pl.when(s < 2)(lambda: add(0, wgu, accx))
        pl.when(s >= 2)(lambda: add(1, wd, accg))

    def lblock(dz, dy):
        return lmat.at[zh if dz == 0 else 1 - zh, c, (y + dy) % 4]

    def l_spread(dz):
        send(lblock(dz, 0), yp, 3, ("ly", dz))
        send(lblock(dz, 0), ym, 3, ("ly", dz))

    def l_on_y(dz):
        landed(lmat.at[0, 0, pl.ds(0, 2)], ("ly", dz))
        send(lblock(dz, 3), yp, 3, ("ly2", dz))

    def lgroup(dz, cc):
        return lmat.at[zh if dz == 0 else 1 - zh, cc]

    def l_sibling(dz):
        landed(lblock(dz, 2), ("ly2", dz))
        send(lgroup(dz, c), sib, 4, ("lc", dz))

    def l_done(dz):
        landed(lgroup(dz, 1 - c), ("lc", dz))

    def greet(k):
        pl.semaphore_signal(met.at[k], inc=1, device_id=zp, device_id_type=MESH)
        pl.semaphore_signal(met.at[k], inc=1, device_id=zm, device_id_type=MESH)

    def greeted(k):
        pl.semaphore_wait(met.at[k], 2)

    def halves(quarter):
        return (2 * quarter, 2 * quarter + 1)

    def on_y_both(dz, quarter):
        for s in halves(quarter):
            on_y(dz, s)

    def on_y2(dz, quarter):
        landed(xg.at[0, 0, 0, 0, :, pl.ds(0, 1024)], ("y2", dz, quarter))
        for s in halves(quarter):
            share_x(dz, "2", s)
        to_sibling(dz, 0, quarter)

    def on_x_all(dz, quarter):
        if (dz, quarter) == (1, 3):
            for s in halves(3):
                landed(xg.at[0, 0, 0, pl.ds(0, 3), :, pl.ds(0, 512)], ("x", 1, s - 3))
                ref = xg.at[1, 1 - zh, c, :, :, eighth(1, s)]
                pltpu.make_async_remote_copy(
                    ref, ref, sent_sem.at[1], in_sem.at[15], device_id=sib, device_id_type=MESH).start()
            return
        landed(xg.at[0, 0, 0, pl.ds(0, 3), :, pl.ds(0, 1024)], ("x", dz, quarter))
        to_sibling(dz, 1, quarter)

    def l_edge():
        at_edge(lambda: lblock(1, 0), inn, 5, ("lz",), arrived=("lz",))

    def l_on_z():
        pl.when(~edge)(lambda: landed(lblock(1, 0), ("lz",)))
        l_spread(1)

    def own(quarter):
        for s in halves(quarter):
            spread_y(0, s)
            at_edge(lambda s=s: piece(0, 0, 0, s), outn, 2, ("z", s), given(0, s))

    def own_rest(quarter):
        cols = quarter_of(1, quarter)
        at_edge(lambda: xg.at[quarter // 2, zh, c, y, :, cols], outn, 2, ("z1", quarter), (tok, cot)[quarter // 2].at[:, cols])

    def other(quarter):
        for s in halves(quarter):
            z_in(s)
            spread_y(1, s)

    half = lax.broadcasted_iota(jnp.int32, (8, 256), 0) < 4

    def over_experts(v, op):
        t = op(v, axis=0)
        a = op(t[0:4], axis=0, keepdims=True)
        b = op(t[4:8], axis=0, keepdims=True)
        return jnp.where(half, a, b)

    def local_scores(dz):
        g = accx[dz, 0:384, :]
        hidden = g / (1.0 + jnp.exp(-g)) * accx[dz, 384:768, :]
        both = hidden * accg[dz]
        return jnp.concatenate([jnp.sum(both[k * 96 : k * 96 + 96], axis=0, keepdims=True) for k in range(4)], axis=0)

    def softmax():
        l_done(0)
        l_done(1)
        for zz in range(2):
            flipped = lmat[zz].reshape(256, 128).T
            for k in range(16):
                probs[k, pl.ds(zz * 4, 4), :] = flipped[k * 4 : k * 4 + 4]
                chosen[k, pl.ds(zz * 4, 4), :] = flipped[64 + k * 4 : 68 + k * 4]
        raw = probs[...]
        raised = jnp.exp(raw - over_experts(raw, jnp.max))
        probs[...] = raised / over_experts(raised, jnp.sum)

    pl.semaphore_wait(barrier, 7)
    own(0)
    own(1)
    for cp in (own_x, own_g, w_gate, w_up, w_down):
        cp.start()
    expert = lax.broadcasted_iota(jnp.int32, (64, 32), 0)
    picked = jnp.zeros((64, 32), jnp.float32)
    for k in range(8):
        picked += (routes[k : k + 1, :] == expert).astype(jnp.float32)
    lmat[zh, c, y, :, pl.ds(0, 64)] = logits[...]
    lmat[zh, c, y, :, pl.ds(64, 64)] = picked.T
    l_spread(0)
    at_edge(lambda: lblock(0, 0), outn, 5, ("lz",))
    own(2)
    own(3)
    for s in range(4):
        own_rest(s)
    greet(0)
    accx[...] = jnp.zeros_like(accx)
    accg[...] = jnp.zeros_like(accg)
    own_x.wait()
    own_g.wait()
    on_y_both(0, 0)
    z_edge(0, 0)
    on_y_both(0, 1)
    z_edge(0, 1)
    l_edge()
    greeted(0)
    greet(1)
    on_y_both(0, 2)
    z_edge(0, 2)
    l_on_y(0)
    other(0)
    on_y_both(0, 3)
    z_edge(0, 3)
    other(1)
    l_on_z()
    on_y2(0, 0)
    greeted(1)
    greet(2)
    on_y2(0, 1)
    other(2)
    z_edge(1, 0)
    on_y_both(1, 0)
    on_y2(0, 2)
    other(3)
    z_edge(1, 1)
    w_gate.wait()
    w_up.wait()
    w_down.wait()

    def before_1():
        on_y_both(1, 1)
        on_y2(0, 3)
        z_edge(1, 2)
        l_sibling(0)
        on_x_all(0, 0)

    def before_2():
        z_edge(1, 3)
        on_x_all(0, 1)

    def before_3():
        on_y_both(1, 2)
        on_x_all(0, 2)
        l_on_y(1)

    def before_5():
        on_y_both(1, 3)
        on_y2(1, 0)
        on_x_all(0, 3)

    def before_6():
        on_y2(1, 1)
        greeted(2)
        l_sibling(1)

    def before_8():
        on_y2(1, 2)

    def before_10():
        on_y2(1, 3)
        z_inner(0)
        on_x_all(1, 0)
        softmax()
        early[...] = local_scores(0)

    def before_11():
        z_inner(1)
        on_x_all(1, 1)

    def before_12():
        z_inner(2)
        on_x_all(1, 2)

    def before_13():
        z_inner(3)
        on_x_all(1, 3)

    before = {1: before_1, 2: before_2, 3: before_3, 5: before_5, 6: before_6, 8: before_8,
              10: before_10, 11: before_11, 12: before_12, 13: before_13}

    def at_step(step, low, high):
        if not any(low <= k < high for k in before):
            return
        if high - low == 1:
            before[low]()
            return
        mid = (low + high) // 2
        lax.cond(step < mid, lambda: at_step(step, low, mid), lambda: at_step(step, mid, high))

    @pl.loop(0, 16)
    def _(step):
        at_step(step, 0, 16)
        multiply(jnp.where(step == 11, 12, jnp.where(step == 12, 11, step)))

    here, there = early[...], local_scores(1)
    part[...] = jnp.where(zh == 0, jnp.concatenate([here, there], 0), jnp.concatenate([there, here], 0))

    def exchange(kind, source, place, peers):
        for k, to in peers:
            pltpu.make_async_remote_copy(
                source, place(k), sent_sem.at[kind], recv_sem[("t", kind)], device_id=to, device_id_type=MESH).start()

    exchange(6, part, lambda k: got_y.at[k], [
        (dy * 2 + dc, dev(x, (y + dy) % 4, z, (c + dc) % 2)) for dy, dc in ((2, 1), (2, 0), (1, 1), (3, 1), (1, 0), (3, 0), (0, 1))])
    landed(got_y.at[pl.ds(1, 7)], ("t", 6))
    total[...] = part[...] + sum(got_y[k] for k in range(1, 8))
    exchange(7, total, lambda k: got_z.at[k], [(k, dev(x, y, (z + k) % 8, c)) for k in (4, 3, 5, 2, 6, 1, 7)])
    landed(got_z.at[pl.ds(1, 7)], ("t", 7))
    for k in range(4):
        first = total[...] if k == 0 else got_z[k]
        got2[x * 4 + (z + 8 - k) % 4] = first + got_z[k + 4]
    mine = got2.at[pl.ds(x * 4, 4)]
    exchange(8, mine, lambda k: mine, [(k, dev((x + k) % 4, y, z, c)) for k in (2, 1, 3)])
    landed(got2.at[pl.ds(0, 12)], ("t", 8))

    scores = got2[...]
    pr, ch = probs[...], chosen[...]
    kept = pr * ch
    mass = over_experts(kept, jnp.sum)
    weighted = over_experts(kept * scores, jnp.sum)
    prob_grad = scores / mass - ch * (weighted / (mass * mass))
    grad = pr * (prob_grad - over_experts(pr * prob_grad, jnp.sum))
    for k in range(16):
        lgc[0, pl.ds(k * 4, 4), :] = grad[k, 0:4]
        lgc[1, pl.ds(k * 4, 4), :] = grad[k, 4:8]
    turned[...] = lgc[zh].T
    lg_out[...] = turned[pl.ds(c * 128 + y * 32, 32), :]
    cols = pl.ds(pl.multiple_of(d * 256, 256), 256)
    rg = jnp.zeros((64, 256), jnp.float32)
    for zz in range(2):
        rows = xg[0, zz, :, :, :, cols].reshape(256, 256)
        rg += jnp.dot(lgc[zz].astype(jnp.bfloat16), rows, preferred_element_type=jnp.float32)
    rg_out[...] = rg

    sent(wd, 0)
    sent(xg.at[0], 1)
    sent(got2.at[pl.ds(0, 12)], 3)
    sent(got2, 4)
    sent(got_y.at[pl.ds(1, 7)], 6)
    sent(got_z.at[pl.ds(1, 7)], 7)
    sent(got2.at[pl.ds(0, 12)], 8)

    @pl.when(edge)
    def _():
        sent(xg.at[0, 0, 0], 2)
        sent(got2.at[pl.ds(0, 4)], 5)


N_RECV = 55


def finish(lg, rg, lg_out, rg_out):
    lg_out[...] = lg[...]
    rg_out[...] = rg[...]


def per_device(tokens, cotangent, logits, routes, gate_weight, up_weight, down_weight):
    flat = [w.reshape(384, 4096) for w in (gate_weight, up_weight, down_weight)]
    hbm, vmem = pl.BlockSpec(memory_space=pl.ANY), pl.BlockSpec(memory_space=pltpu.VMEM)
    f32, bf16 = jnp.float32, jnp.bfloat16
    logit_grad, router_grad = pl.pallas_call(
        kernel,
        out_shape=(pltpu.VMEM((32, 64), f32), pltpu.VMEM((64, 256), f32)),
        in_specs=[hbm, hbm, vmem, vmem, hbm, hbm, hbm],
        out_specs=(vmem, vmem),
        scratch_shapes=[
            pltpu.VMEM((2, 2, 2, 4, 32, 4096), bf16),
            pltpu.VMEM((768, 4096), bf16),
            pltpu.VMEM((384, 4096), bf16),
            pltpu.VMEM((2, 768, 256), f32),
            pltpu.VMEM((2, 384, 256), f32),
            pltpu.VMEM((2, 2, 4, 32, 128), f32),
            pltpu.VMEM((16, 8, 256), f32),
            pltpu.VMEM((16, 8, 256), f32),
            pltpu.VMEM((4, 256), f32),
            pltpu.VMEM((8, 256), f32),
            pltpu.VMEM((8, 256), f32),
            pltpu.VMEM((8, 8, 256), f32),
            pltpu.VMEM((8, 8, 256), f32),
            pltpu.VMEM((16, 8, 256), f32),
            pltpu.VMEM((2, 64, 256), f32),
            pltpu.VMEM((256, 64), f32),
            pltpu.SemaphoreType.DMA((5,)),
            pltpu.SemaphoreType.DMA((9,)),
            pltpu.SemaphoreType.DMA((N_RECV,)),
            pltpu.SemaphoreType.DMA((16,)),
            pltpu.SemaphoreType.REGULAR((3,)),
        ],
        compiler_params=pltpu.CompilerParams(
            collective_id=0, has_side_effects=True, vmem_limit_bytes=60 * MIB),
        cost_estimate=pl.CostEstimate(flops=2 * 512 * 384 * 4096 * 3, bytes_accessed=10 * MIB, transcendentals=512 * 384),
        name="router_grad",
    )(tokens, cotangent, logits, routes.T, *flat)
    logit_grad, router_grad = pl.pallas_call(
        finish,
        out_shape=(jax.ShapeDtypeStruct((32, 64), f32), jax.ShapeDtypeStruct((64, 256), f32)),
        in_specs=[vmem, vmem],
        out_specs=(vmem, vmem),
        name="finish",
    )(*(pltpu.with_memory_space_constraint(v, pltpu.VMEM) for v in (logit_grad, router_grad)))
    return logit_grad, router_grad.T


def solution(mesh):
    rows = P("dp", None)
    placed = (rows, rows, rows, rows) + (P("expert", "dp", None),) * 3
    return jax.shard_map(
        per_device, mesh=mesh, in_specs=placed, out_specs=(rows, rows), check_vma=False)
```

```python
import jax
import jax.numpy as jnp
from jax import lax
from jax.experimental import pallas as pl
from jax.experimental.pallas import tpu as pltpu
from jax.sharding import PartitionSpec as P

MESH = pl.DeviceIdType.MESH
MIB = 1024 * 1024
NT = (((1,), (1,)), ((), ()))


class Sems:
    def __init__(self, ref):
        self.ref, self.names = ref, {}

    def __getitem__(self, name):
        k = self.names.setdefault(name, len(self.names))
        assert k < N_RECV
        return self.ref.at[k]


def kernel(tok, cot, logits, routes, gate, up, down, lg_out, rg_out,
           xg, wgu, wd, accx, accg, lmat, probs, chosen, early, part, total, got_y, got_z, got2, lgc, turned,
           load_sem, sent_sem, recv_ref, in_sem, met):
    d = lax.axis_index("dp")
    e = lax.axis_index("expert")
    y, zh, c = d // 4, (d // 2) % 2, d % 2
    x, zl = e // 4, e % 4
    z = zh * 4 + zl
    par = x % 2
    recv_sem = Sems(recv_ref)

    def dev(x_, y_, z_, c_):
        return ((y_ * 2 + z_ // 4) * 2 + c_, x_ * 4 + z_ % 4)

    xp, xm = dev((x + 1) % 4, y, z, c), dev((x + 3) % 4, y, z, c)
    yp, ym = dev(x, (y + 1) % 4, z, c), dev(x, (y + 3) % 4, z, c)
    zp, zm = dev(x, y, (z + 1) % 8, c), dev(x, y, (z + 7) % 8, c)
    low = zl < 2
    outn = tuple(jnp.where(low, a, b) for a, b in zip(zm, zp))
    inn = tuple(jnp.where(low, a, b) for a, b in zip(zp, zm))
    sib = dev(x, y, z, 1 - c)
    edge = (zl == 0) | (zl == 3)

    barrier = pltpu.get_barrier_semaphore()
    for to in (yp, ym, xp, xm, zp, zm, sib):
        pl.semaphore_signal(barrier, inc=1, device_id=to, device_id_type=MESH)
    own_x = pltpu.make_async_copy(tok, xg.at[0, zh, c, y], load_sem.at[0])
    own_g = pltpu.make_async_copy(cot, xg.at[1, zh, c, y], load_sem.at[1])
    w_gate = pltpu.make_async_copy(gate, wgu.at[pl.ds(0, 384)], load_sem.at[2])
    w_up = pltpu.make_async_copy(up, wgu.at[pl.ds(384, 384)], load_sem.at[3])
    w_down = pltpu.make_async_copy(down, wd, load_sem.at[4])


    def send(ref, to, kind, name_there, source=None):
        pltpu.make_async_remote_copy(
            ref if source is None else source, ref, sent_sem.at[kind], recv_sem[name_there],
            device_id=to, device_id_type=MESH).start()

    def landed(ref, name):
        pltpu.make_async_remote_copy(
            ref, ref, sent_sem.at[0], recv_sem[name], device_id=sib, device_id_type=MESH).wait_recv()

    def sent(ref, kind):
        pltpu.make_async_remote_copy(
            ref, ref, sent_sem.at[kind], recv_sem[("lz",)], device_id=sib, device_id_type=MESH).wait_send()

    def eighth(rel, s):
        q = 2 * (s // 2 % 2) + (par if rel == 0 else 1 - par)
        return pl.ds(pl.multiple_of(q * 1024 + s % 2 * 512, 512), 512)

    def piece(dz, dy, rel, s):
        zz = zh if dz == 0 else 1 - zh
        return xg.at[s // 4, zz, c, (y + dy) % 4, :, eighth(rel, s)]

    def group(dz, rel, s, cc):
        zz = zh if dz == 0 else 1 - zh
        q = 2 * (s % 2) + (par if rel == 0 else 1 - par)
        return xg.at[s // 2, zz, cc, :, :, pl.ds(pl.multiple_of(q * 1024, 1024), 1024)]

    DY = {"m": 3, "p": 1, "2": 2}

    def given(rel, s):
        return (tok, cot)[s // 4].at[:, eighth(rel, s)]

    def spread_y(dz, s):
        source = given(0, s) if dz == 0 else None
        send(piece(dz, 0, 0, s), yp, 0, ("y", dz, s), source)
        send(piece(dz, 0, 0, s), ym, 0, ("y", dz, s), source)

    def share_x(dz, who, s):
        forward = {"m": True, "p": False, "2": s % 2 == 0}[who]
        forward = forward if s < 4 else not forward
        send(piece(dz, DY[who], 0, s), xp if forward else xm, 0, ("x", dz, s // 2 if (dz, s) != (1, 7) else 4))

    def on_y(dz, s):
        landed(xg.at[0, 0, 0, 0, :, pl.ds(0, 1024)], ("y", dz, s))
        who, to = ("m", yp) if s % 2 == 0 else ("p", ym)
        send(piece(dz, DY[who], 0, s), to, 0, ("y2", dz, s // 2))
        share_x(dz, "m", s)
        share_x(dz, "p", s)

    def at_edge(like, to, kind, name_there, source=None, arrived=None):
        @pl.when(edge)
        def _():
            if arrived is not None:
                landed(like(), arrived)
            send(like(), to, kind, name_there, source)

    def quarter_of(rel, quarter):
        q = 2 * (quarter % 2) + (par if rel == 0 else 1 - par)
        return pl.ds(pl.multiple_of(q * 1024, 1024), 1024)

    def other_own(quarter):
        return xg.at[quarter // 2, 1 - zh, c, y, :, quarter_of(1, quarter)]

    def z_edge(rel, quarter):
        if rel == 1:
            at_edge(lambda: other_own(quarter), inn, 2, ("z1", quarter), arrived=("z1", quarter))
            return
        for s in (2 * quarter, 2 * quarter + 1):
            at_edge(lambda s=s: piece(1, 0, 0, s), inn, 2, ("z", s), arrived=("z", s))

    def z_in(s):
        pl.when(~edge)(lambda: landed(piece(1, 0, 0, s), ("z", s)))

    def z_inner(quarter):
        pl.when(~edge)(lambda: landed(other_own(quarter), ("z1", quarter)))

    def to_sibling(dz, rel, s):
        k = dz * 8 + rel * 4 + s
        cp = pltpu.make_async_remote_copy(
            group(dz, rel, s, c), group(dz, rel, s, c), sent_sem.at[1], in_sem.at[k], device_id=sib, device_id_type=MESH)
        cp.start()

    def multiply(step):
        dz, rel, s = step // 8, step // 4 % 2, step % 4
        zz = jnp.where(dz == 0, zh, 1 - zh)
        q = 2 * (s % 2) + jnp.where(rel == 0, par, 1 - par)
        cols = pl.ds(pl.multiple_of(q * 1024, 1024), 1024)
        arrived = xg.at[s // 2, zz, 1 - c, :, :, cols]
        pltpu.make_async_remote_copy(
            arrived, arrived, sent_sem.at[1], in_sem.at[step], device_id=sib, device_id_type=MESH).wait_recv()

        def add(arr, w, acc):
            rows = xg[arr, zz, :, :, :, cols].reshape(256, 1024)
            size = 256 if arr == 0 else 384
            for m in range(0, w.shape[0], size):
                at = pl.ds(m, size)
                acc[dz, at, :] += lax.dot_general(w[at, cols], rows, NT, preferred_element_type=jnp.float32)

        pl.when(s < 2)(lambda: add(0, wgu, accx))
        pl.when(s >= 2)(lambda: add(1, wd, accg))

    def lblock(dz, dy):
        return lmat.at[zh if dz == 0 else 1 - zh, c, (y + dy) % 4]

    def l_spread(dz):
        send(lblock(dz, 0), yp, 3, ("ly", dz))
        send(lblock(dz, 0), ym, 3, ("ly", dz))

    def l_on_y(dz):
        landed(lmat.at[0, 0, pl.ds(0, 2)], ("ly", dz))
        send(lblock(dz, 3), yp, 3, ("ly2", dz))

    def lgroup(dz, cc):
        return lmat.at[zh if dz == 0 else 1 - zh, cc]

    def l_sibling(dz):
        landed(lblock(dz, 2), ("ly2", dz))
        send(lgroup(dz, c), sib, 4, ("lc", dz))

    def l_done(dz):
        landed(lgroup(dz, 1 - c), ("lc", dz))

    def greet(k):
        pl.semaphore_signal(met.at[k], inc=1, device_id=zp, device_id_type=MESH)
        pl.semaphore_signal(met.at[k], inc=1, device_id=zm, device_id_type=MESH)

    def greeted(k):
        pl.semaphore_wait(met.at[k], 2)

    def halves(quarter):
        return (2 * quarter, 2 * quarter + 1)

    def on_y_both(dz, quarter):
        for s in halves(quarter):
            on_y(dz, s)

    def on_y2(dz, quarter):
        landed(xg.at[0, 0, 0, 0, :, pl.ds(0, 1024)], ("y2", dz, quarter))
        for s in halves(quarter):
            share_x(dz, "2", s)
        to_sibling(dz, 0, quarter)

    def on_x_all(dz, quarter):
        if (dz, quarter) == (1, 3):
            for s in halves(3):
                landed(xg.at[0, 0, 0, pl.ds(0, 3), :, pl.ds(0, 512)], ("x", 1, s - 3))
                ref = xg.at[1, 1 - zh, c, :, :, eighth(1, s)]
                pltpu.make_async_remote_copy(
                    ref, ref, sent_sem.at[1], in_sem.at[15], device_id=sib, device_id_type=MESH).start()
            return
        landed(xg.at[0, 0, 0, pl.ds(0, 3), :, pl.ds(0, 1024)], ("x", dz, quarter))
        to_sibling(dz, 1, quarter)

    def l_edge():
        at_edge(lambda: lblock(1, 0), inn, 5, ("lz",), arrived=("lz",))

    def l_on_z():
        pl.when(~edge)(lambda: landed(lblock(1, 0), ("lz",)))
        l_spread(1)

    def own(quarter):
        for s in halves(quarter):
            spread_y(0, s)
            at_edge(lambda s=s: piece(0, 0, 0, s), outn, 2, ("z", s), given(0, s))

    def own_rest(quarter):
        cols = quarter_of(1, quarter)
        at_edge(lambda: xg.at[quarter // 2, zh, c, y, :, cols], outn, 2, ("z1", quarter), (tok, cot)[quarter // 2].at[:, cols])

    def other(quarter):
        for s in halves(quarter):
            z_in(s)
            spread_y(1, s)

    half = lax.broadcasted_iota(jnp.int32, (8, 256), 0) < 4

    def over_experts(v, op):
        t = op(v, axis=0)
        a = op(t[0:4], axis=0, keepdims=True)
        b = op(t[4:8], axis=0, keepdims=True)
        return jnp.where(half, a, b)

    def local_scores(dz):
        g = accx[dz, 0:384, :]
        hidden = g / (1.0 + jnp.exp(-g)) * accx[dz, 384:768, :]
        both = hidden * accg[dz]
        return jnp.concatenate([jnp.sum(both[k * 96 : k * 96 + 96], axis=0, keepdims=True) for k in range(4)], axis=0)

    def softmax():
        l_done(0)
        l_done(1)
        for zz in range(2):
            flipped = lmat[zz].reshape(256, 128).T
            for k in range(16):
                probs[k, pl.ds(zz * 4, 4), :] = flipped[k * 4 : k * 4 + 4]
                chosen[k, pl.ds(zz * 4, 4), :] = flipped[64 + k * 4 : 68 + k * 4]
        raw = probs[...]
        raised = jnp.exp(raw - over_experts(raw, jnp.max))
        probs[...] = raised / over_experts(raised, jnp.sum)

    pl.semaphore_wait(barrier, 7)
    own(0)
    own(1)
    for cp in (own_x, own_g, w_gate, w_up, w_down):
        cp.start()
    expert = lax.broadcasted_iota(jnp.int32, (64, 32), 0)
    picked = jnp.zeros((64, 32), jnp.float32)
    for k in range(8):
        picked += (routes[k : k + 1, :] == expert).astype(jnp.float32)
    lmat[zh, c, y, :, pl.ds(0, 64)] = logits[...]
    lmat[zh, c, y, :, pl.ds(64, 64)] = picked.T
    l_spread(0)
    at_edge(lambda: lblock(0, 0), outn, 5, ("lz",))
    own(2)
    own(3)
    for s in range(4):
        own_rest(s)
    greet(0)
    accx[...] = jnp.zeros_like(accx)
    accg[...] = jnp.zeros_like(accg)
    own_x.wait()
    own_g.wait()
    on_y_both(0, 0)
    z_edge(0, 0)
    on_y_both(0, 1)
    z_edge(0, 1)
    l_edge()
    greeted(0)
    greet(1)
    on_y_both(0, 2)
    z_edge(0, 2)
    l_on_y(0)
    other(0)
    on_y_both(0, 3)
    z_edge(0, 3)
    other(1)
    l_on_z()
    on_y2(0, 0)
    greeted(1)
    greet(2)
    on_y2(0, 1)
    other(2)
    z_edge(1, 0)
    on_y_both(1, 0)
    on_y2(0, 2)
    other(3)
    z_edge(1, 1)
    w_gate.wait()
    w_up.wait()
    w_down.wait()

    def before_1():
        on_y_both(1, 1)
        on_y2(0, 3)
        z_edge(1, 2)
        l_sibling(0)
        on_x_all(0, 0)

    def before_2():
        z_edge(1, 3)
        on_x_all(0, 1)

    def before_3():
        on_y_both(1, 2)
        on_x_all(0, 2)
        l_on_y(1)

    def before_5():
        on_y_both(1, 3)
        on_y2(1, 0)
        on_x_all(0, 3)

    def before_6():
        on_y2(1, 1)
        greeted(2)
        l_sibling(1)

    def before_8():
        on_y2(1, 2)

    def before_10():
        on_y2(1, 3)
        z_inner(0)
        on_x_all(1, 0)
        softmax()
        early[...] = local_scores(0)

    def before_11():
        z_inner(1)
        on_x_all(1, 1)

    def before_12():
        z_inner(2)
        on_x_all(1, 2)

    def before_13():
        z_inner(3)
        on_x_all(1, 3)

    before = {1: before_1, 2: before_2, 3: before_3, 5: before_5, 6: before_6, 8: before_8,
              10: before_10, 11: before_11, 12: before_12, 13: before_13}

    def at_step(step, low, high):
        if not any(low <= k < high for k in before):
            return
        if high - low == 1:
            before[low]()
            return
        mid = (low + high) // 2
        lax.cond(step < mid, lambda: at_step(step, low, mid), lambda: at_step(step, mid, high))

    @pl.loop(0, 16)
    def _(step):
        at_step(step, 0, 16)
        multiply(jnp.where(step == 11, 12, jnp.where(step == 12, 11, step)))

    here, there = early[...], local_scores(1)
    part[...] = jnp.where(zh == 0, jnp.concatenate([here, there], 0), jnp.concatenate([there, here], 0))

    def exchange(kind, source, place, peers):
        for k, to in peers:
            pltpu.make_async_remote_copy(
                source, place(k), sent_sem.at[kind], recv_sem[("t", kind)], device_id=to, device_id_type=MESH).start()

    exchange(6, part, lambda k: got_y.at[k], [
        (dy * 2 + dc, dev(x, (y + dy) % 4, z, (c + dc) % 2)) for dy, dc in ((2, 1), (2, 0), (1, 1), (3, 1), (1, 0), (3, 0), (0, 1))])
    landed(got_y.at[pl.ds(1, 7)], ("t", 6))
    total[...] = part[...] + sum(got_y[k] for k in range(1, 8))
    for k in (4, 2, 6, 3, 5, 1, 7):
        pltpu.make_async_remote_copy(
            total, got_z.at[k], sent_sem.at[7], recv_sem[("tz", k % 4)],
            device_id=dev(x, y, (z + k) % 8, c), device_id_type=MESH).start()
    for k in (2, 1, 3, 0):
        landed(got_z.at[pl.ds(0, 2 if k else 1)], ("tz", k))
        first = total[...] if k == 0 else got_z[k]
        place = x * 4 + (z + 8 - k) % 4
        got2[place] = first + got_z[k + 4]
        mine = got2.at[place]
        exchange(8, mine, lambda j: mine, [(j, dev((x + j) % 4, y, z, c)) for j in (2, 1, 3)])
    landed(got2.at[pl.ds(0, 12)], ("t", 8))

    scores = got2[...]
    pr, ch = probs[...], chosen[...]
    kept = pr * ch
    mass = over_experts(kept, jnp.sum)
    weighted = over_experts(kept * scores, jnp.sum)
    prob_grad = scores / mass - ch * (weighted / (mass * mass))
    grad = pr * (prob_grad - over_experts(pr * prob_grad, jnp.sum))
    for k in range(16):
        lgc[0, pl.ds(k * 4, 4), :] = grad[k, 0:4]
        lgc[1, pl.ds(k * 4, 4), :] = grad[k, 4:8]
    turned[...] = lgc[zh].T
    lg_out[...] = turned[pl.ds(c * 128 + y * 32, 32), :]
    cols = pl.ds(pl.multiple_of(d * 256, 256), 256)
    rg = jnp.zeros((64, 256), jnp.float32)
    for zz in range(2):
        rows = xg[0, zz, :, :, :, cols].reshape(256, 256)
        rg += jnp.dot(lgc[zz].astype(jnp.bfloat16), rows, preferred_element_type=jnp.float32)
    rg_out[...] = rg

    sent(wd, 0)
    sent(xg.at[0], 1)
    sent(got2.at[pl.ds(0, 12)], 3)
    sent(got2, 4)
    sent(got_y.at[pl.ds(1, 7)], 6)
    sent(got_z.at[pl.ds(1, 7)], 7)
    sent(got2.at[pl.ds(0, 12)], 8)

    @pl.when(edge)
    def _():
        sent(xg.at[0, 0, 0], 2)
        sent(got2.at[pl.ds(0, 4)], 5)


N_RECV = 58


def finish(lg, rg, lg_out, rg_out):
    lg_out[...] = lg[...]
    rg_out[...] = rg[...]


def per_device(tokens, cotangent, logits, routes, gate_weight, up_weight, down_weight):
    flat = [w.reshape(384, 4096) for w in (gate_weight, up_weight, down_weight)]
    hbm, vmem = pl.BlockSpec(memory_space=pl.ANY), pl.BlockSpec(memory_space=pltpu.VMEM)
    f32, bf16 = jnp.float32, jnp.bfloat16
    logit_grad, router_grad = pl.pallas_call(
        kernel,
        out_shape=(pltpu.VMEM((32, 64), f32), pltpu.VMEM((64, 256), f32)),
        in_specs=[hbm, hbm, vmem, vmem, hbm, hbm, hbm],
        out_specs=(vmem, vmem),
        scratch_shapes=[
            pltpu.VMEM((2, 2, 2, 4, 32, 4096), bf16),
            pltpu.VMEM((768, 4096), bf16),
            pltpu.VMEM((384, 4096), bf16),
            pltpu.VMEM((2, 768, 256), f32),
            pltpu.VMEM((2, 384, 256), f32),
            pltpu.VMEM((2, 2, 4, 32, 128), f32),
            pltpu.VMEM((16, 8, 256), f32),
            pltpu.VMEM((16, 8, 256), f32),
            pltpu.VMEM((4, 256), f32),
            pltpu.VMEM((8, 256), f32),
            pltpu.VMEM((8, 256), f32),
            pltpu.VMEM((8, 8, 256), f32),
            pltpu.VMEM((8, 8, 256), f32),
            pltpu.VMEM((16, 8, 256), f32),
            pltpu.VMEM((2, 64, 256), f32),
            pltpu.VMEM((256, 64), f32),
            pltpu.SemaphoreType.DMA((5,)),
            pltpu.SemaphoreType.DMA((9,)),
            pltpu.SemaphoreType.DMA((N_RECV,)),
            pltpu.SemaphoreType.DMA((16,)),
            pltpu.SemaphoreType.REGULAR((3,)),
        ],
        compiler_params=pltpu.CompilerParams(
            collective_id=0, has_side_effects=True, vmem_limit_bytes=60 * MIB),
        cost_estimate=pl.CostEstimate(flops=2 * 512 * 384 * 4096 * 3, bytes_accessed=10 * MIB, transcendentals=512 * 384),
        name="router_grad",
    )(tokens, cotangent, logits, routes.T, *flat)
    logit_grad, router_grad = pl.pallas_call(
        finish,
        out_shape=(jax.ShapeDtypeStruct((32, 64), f32), jax.ShapeDtypeStruct((64, 256), f32)),
        in_specs=[vmem, vmem],
        out_specs=(vmem, vmem),
        name="finish",
    )(*(pltpu.with_memory_space_constraint(v, pltpu.VMEM) for v in (logit_grad, router_grad)))
    return logit_grad, router_grad.T


def solution(mesh):
    rows = P("dp", None)
    placed = (rows, rows, rows, rows) + (P("expert", "dp", None),) * 3
    return jax.shard_map(
        per_device, mesh=mesh, in_specs=placed, out_specs=(rows, rows), check_vma=False)
```
